32 devices in a mesh: groups: 2 (over y), batch: 4 (over z), tensor: 4 (over x, core).
Axes of the slice: x: 2, y: 2, z: 4, core: 2. Of those that a mesh axis runs over, the one named last changes fastest.
Arguments:
- queries: bfloat16 [768, 8192], P(('groups', 'batch'), 'tensor'), parts along dimension 0, may hold values from -88 to 88, as said below
- cached_keys: bfloat16 [768, 64, 1024], P(('groups', 'batch'), None, 'tensor'), parts along dimension 0, may hold values from -4 to 4, as said below
- cached_values: bfloat16 [768, 64, 1024], P(('groups', 'batch'), None, 'tensor'), parts along dimension 0, may hold values from -5 to 5
- token_key: bfloat16 [768, 1024], P(('groups', 'batch'), 'tensor'), parts along dimension 0, may hold values from -5 to 5
- token_value: bfloat16 [768, 1024], P(('groups', 'batch'), 'tensor'), parts along dimension 0, may hold values from -5 to 5
- lengths: int32 [768], P(('groups', 'batch')), parts along dimension 0, may hold values from 2 to 64
- adapter_index: int32 [768], P(('groups', 'batch')), parts along dimension 0, may hold values from 0 to 15, as said below
- output_weight: bfloat16 [8192, 8192], P('tensor', 'batch'), may hold values from -0.0625 to 0.0625
- adapter_down: bfloat16 [16, 8192, 64], P('batch', 'tensor'), may hold values from -0.0625 to 0.0625
- adapter_up: bfloat16 [16, 64, 8192], P('batch', None, 'tensor'), may hold values from -0.75 to 0.75
Outputs:
- projected: bfloat16 [768, 8192], P(('groups', 'batch'), 'tensor'), parts along dimension 0
The draws below stay inside these ranges and needn't reach their ends.
There are 2 independent parts, one for each index of `groups`. The reference program is written for one: setup_inputs(seed, part) draws one part's arguments, and reference() takes and returns one part's arrays. A program takes and returns all parts, laid end to end along the dimension named above; an argument that names none is the same for every part. Nothing has to cross between parts.
Inputs may be any that keep to these rules, and one draw needn't show every extreme that they name: `queries`: entries of order one; in some requests every head's query is a multiple of 10 to 22 of the request's first cached key of that head's key-value head. `cached_keys`: the second cached key of each request is 0.99 times its first. `adapter_index`: device blocks are the aligned runs of 96 requests; owner o holds adapters 4 * o to 4 * o + 3. No block has more than 48 requests on adapters of one owner, and in every draw some owner receives exactly 48 from every block.
All inputs are finite; a program needn't handle non-finite values.
Results may differ from the reference program's by a relative error of at most 0.0057.
Values may be sent and summed in bfloat16 or wider, within the bound.
A program may use at most 64 MiB of HBM per device.

```python
import jax
import jax.numpy as jnp
from jax import lax

MODEL_WIDTH = 8192
QUERY_HEADS = 64
KVH = 8
HEAD_SIZE = 128
ADAPTER_RANK = 64
BATCH_REQUESTS = 96
LMAX = 64
ADAPT_DEV = 4
REQUEST_TOTAL = 384
ADAPTER_TOTAL = 16
N_BATCH = 4


def first_keys(key):
    return jnp.clip(jax.random.normal(key, (REQUEST_TOTAL, KVH * HEAD_SIZE), jnp.float32), -4.0, 4.0)


def draw_cached_keys(key, part):
    first = first_keys(key)
    key = jax.random.fold_in(key, 11)
    others = jnp.clip(jax.random.normal(key, (REQUEST_TOTAL, LMAX - 2, KVH * HEAD_SIZE), jnp.float32), -4.0, 4.0)
    whole = jnp.concatenate([first[:, None, :], 0.99 * first[:, None, :], others], axis=1)
    return whole.astype(jnp.bfloat16)


def draw_queries(key, part):
    first = first_keys(key)
    key = jax.random.fold_in(key, 23)
    key_drawn, key_pick, key_level = jax.random.split(key, 3)
    drawn = jnp.clip(jax.random.normal(key_drawn, (REQUEST_TOTAL, QUERY_HEADS * HEAD_SIZE), jnp.float32), -4.0, 4.0)
    picked = jax.random.bernoulli(key_pick, 0.125, (REQUEST_TOTAL,))
    level = jax.random.randint(key_level, (REQUEST_TOTAL,), 0, 3).astype(jnp.float32)
    strength = 10.0 + 6.0 * level
    aligned = jnp.broadcast_to(first.reshape(REQUEST_TOTAL, KVH, 1, HEAD_SIZE), (REQUEST_TOTAL, KVH, QUERY_HEADS // KVH, HEAD_SIZE))
    aligned = aligned.reshape(REQUEST_TOTAL, QUERY_HEADS * HEAD_SIZE) * strength[:, None]
    return jnp.where(picked[:, None], aligned, drawn).astype(jnp.bfloat16)


def draw_adapter_index(key, part):
    key = jax.random.fold_in(key, 5)
    most = max(2, 2 * BATCH_REQUESTS // N_BATCH)
    key_hot, key_rest, key_local = jax.random.split(key, 3)
    hot = jax.random.randint(key_hot, (), 0, N_BATCH)

    def one_block(block_key):
        key_pick, key_order = jax.random.split(block_key)
        picks = jax.random.permutation(key_pick, (N_BATCH - 1) * most)[:BATCH_REQUESTS - most]
        other = picks // most
        other = other + (other >= hot).astype(jnp.int32)
        owners = jnp.concatenate([jnp.full((most,), hot, jnp.int32), other.astype(jnp.int32)])
        return owners[jax.random.permutation(key_order, BATCH_REQUESTS)]
    owners = jax.vmap(one_block)(jax.random.split(key_rest, N_BATCH)).reshape(-1)
    local = jax.random.randint(key_local, (BATCH_REQUESTS * N_BATCH,), 0, ADAPT_DEV)
    return (owners * ADAPT_DEV + local).astype(jnp.int32)


def set_ends(result, key, smallest, largest):
    place = [jax.random.randint(jax.random.fold_in(key, axis), (), 0, length) for axis, length in enumerate(result.shape)]
    main_axis = result.shape.index(max(result.shape))
    neighbour = place[:main_axis] + [(place[main_axis] + 1) % result.shape[main_axis]] + place[main_axis + 1:]
    return result.at[tuple(place)].set(smallest).at[tuple(neighbour)].set(largest)


def shard_levels(key, shape, cuts, least, high):
    def one(axis_at, parts):
        steps = jax.random.uniform(jax.random.fold_in(jax.random.fold_in(key, 6), axis_at), (parts,), jnp.float32, least / len(cuts), high / len(cuts))
        return jnp.repeat(jnp.exp(steps), shape[axis_at] // parts).reshape((-1,) + (1,) * (len(shape) - axis_at - 1))

    factor_of = one(*cuts[0])
    for cut in cuts[1:]:
        factor_of = factor_of * one(*cut)
    return factor_of


def normal_values(stream_key, dims, scale, reach, cuts=(), held_as=jnp.bfloat16):
    entries = jax.random.normal(stream_key, dims, jnp.float32) * scale
    if len(cuts) > 0:
        entries = shard_levels(stream_key, dims, cuts, -0.22, 0.18) * entries
    return jnp.clip(entries, min=-reach, max=reach).astype(held_as)


def setup_inputs(seed: int = 0, part: int = 0) -> dict:
    splits = jax.random.split(jax.random.key(seed), 11)
    part_splits = jax.random.split(jax.random.fold_in(splits[10], part), 11)
    queries = draw_queries(jax.random.fold_in(jax.random.fold_in(splits[10], part), 71), part)
    cached_keys = draw_cached_keys(jax.random.fold_in(jax.random.fold_in(splits[10], part), 71), part)
    cached_values = normal_values(part_splits[2], (REQUEST_TOTAL, LMAX, KVH * HEAD_SIZE), 1.0, 5.0, ((0, 4), (2, 4)))
    token_key = normal_values(part_splits[3], (REQUEST_TOTAL, KVH * HEAD_SIZE), 1.0, 5.0, ((0, 4), (1, 4)))
    token_value = normal_values(part_splits[4], (REQUEST_TOTAL, KVH * HEAD_SIZE), 1.0, 5.0, ((0, 4), (1, 4)))
    lengths = set_ends(jax.random.randint(part_splits[5], (REQUEST_TOTAL,), 2, LMAX + 1), jax.random.fold_in(part_splits[5], 1), 2, LMAX).astype(jnp.int32)
    adapter_index = draw_adapter_index(jax.random.fold_in(jax.random.fold_in(splits[10], part), 71), part)
    output_weight = normal_values(splits[7], (QUERY_HEADS * HEAD_SIZE, MODEL_WIDTH), (QUERY_HEADS * HEAD_SIZE) ** -0.5, 0.0625, ((0, 4), (1, 4)))
    adapter_down = normal_values(splits[8], (ADAPTER_TOTAL, QUERY_HEADS * HEAD_SIZE, ADAPTER_RANK), (QUERY_HEADS * HEAD_SIZE) ** -0.5, 0.0625, ((0, 4), (1, 4)))
    adapter_up = normal_values(splits[9], (ADAPTER_TOTAL, ADAPTER_RANK, MODEL_WIDTH), ADAPTER_RANK ** -0.5, 0.75, ((0, 4), (2, 4)))
    return dict(queries=queries, cached_keys=cached_keys, cached_values=cached_values, token_key=token_key, token_value=token_value, lengths=lengths, adapter_index=adapter_index, output_weight=output_weight, adapter_down=adapter_down, adapter_up=adapter_up)


adapter_scale = 0.25


def attend(items):
    query_rows, keys, values, newest_key, fresh_value, valid_len = items
    count = query_rows.shape[0]
    group = QUERY_HEADS // KVH
    score_scale = HEAD_SIZE ** -0.5
    query_rows = query_rows.astype(jnp.float32).reshape(count, KVH, group, HEAD_SIZE)
    keys = keys.astype(jnp.float32).reshape(count, LMAX, KVH, HEAD_SIZE)
    values = values.astype(jnp.float32).reshape(count, LMAX, KVH, HEAD_SIZE)
    newest_key = newest_key.astype(jnp.float32).reshape(count, KVH, HEAD_SIZE)
    fresh_value = fresh_value.astype(jnp.float32).reshape(count, KVH, HEAD_SIZE)
    scores = jnp.einsum("bkgd,blkd->bkgl", query_rows, keys) * score_scale
    owned_rows = jnp.einsum("prwn,prn->prw", query_rows, newest_key) * score_scale
    valid = jnp.arange(LMAX, dtype=jnp.int32)[None, :] < valid_len[:, None]
    scores = jnp.where(valid[:, None, None, :], scores, -jnp.inf)
    top = jnp.maximum(jnp.max(scores, axis=-1), owned_rows)
    expo = jnp.exp(scores - top[..., None])
    own_expo = jnp.exp(owned_rows - top)
    total = jnp.sum(expo, axis=-1) + own_expo
    weights = (expo / total[..., None]).astype(jnp.bfloat16)
    own_weight = (own_expo / total).astype(jnp.bfloat16)
    weights = lax.optimization_barrier(weights)
    own_weight = lax.optimization_barrier(own_weight)
    mixed = jnp.einsum("bkgl,blkd->bkgd", weights.astype(jnp.float32), values)
    mixed = mixed + own_weight.astype(jnp.float32)[..., None] * fresh_value[:, :, None, :]
    return mixed.reshape(count, QUERY_HEADS * HEAD_SIZE).astype(jnp.bfloat16)


def reference(queries, cached_keys, cached_values, token_key, token_value, lengths, adapter_index, output_weight, adapter_down, adapter_up):
    cache_blocks = REQUEST_TOTAL // BATCH_REQUESTS
    shaped = tuple(arr.reshape((cache_blocks, BATCH_REQUESTS) + arr.shape[1:]) for arr in (queries, cached_keys, cached_values, token_key, token_value, lengths))
    attention_output = lax.map(attend, shaped).reshape(REQUEST_TOTAL, QUERY_HEADS * HEAD_SIZE)
    attention_output = lax.optimization_barrier(attention_output)
    base_output = jnp.dot(attention_output, output_weight, preferred_element_type=jnp.float32)

    def apply_adapter(items):
        rows_in, request_index = items
        down_factor = adapter_down[request_index].astype(jnp.float32)
        small_product = jnp.einsum("rf,rfk->rk", rows_in.astype(jnp.float32), down_factor).astype(jnp.bfloat16)
        small_product = lax.optimization_barrier(small_product)
        up_factor = adapter_up[request_index].astype(jnp.float32)
        return adapter_scale * jnp.einsum("gx,gxd->gd", small_product.astype(jnp.float32), up_factor)

    adapter_delta = lax.map(apply_adapter, (attention_output.reshape(cache_blocks, BATCH_REQUESTS, QUERY_HEADS * HEAD_SIZE), adapter_index.reshape(cache_blocks, BATCH_REQUESTS)))
    adapter_delta = adapter_delta.reshape(REQUEST_TOTAL, MODEL_WIDTH).astype(jnp.bfloat16)
    adapter_delta = lax.optimization_barrier(adapter_delta)
    return (base_output + adapter_delta.astype(jnp.float32)).astype(jnp.bfloat16)
```

```python
import jax
import jax.numpy as jnp
from jax import lax
from jax.experimental import pallas as pl
from jax.experimental.pallas import tpu as pltpu
from jax.sharding import PartitionSpec as P

HEAD_SIZE = 128


adapter_scale = 0.25


def finish_output(
    flattened_rows, select_adapter, adapter_down, adapter_up, owner_count, taken_rows
):
    down_factor = jnp.einsum(
        "tj,ojx->tox", flattened_rows, adapter_down, preferred_element_type=jnp.float32
    )
    partial_small = jnp.einsum("sak,sa->sk", down_factor, select_adapter)
    small_product = lax.psum(partial_small, "tensor").astype(jnp.bfloat16)
    up_factor = jnp.einsum(
        "yg,rgo->yro", small_product, adapter_up, preferred_element_type=jnp.float32
    )
    final_result = (adapter_scale * jnp.einsum("czp,cz->cp", up_factor, select_adapter)).astype(
        jnp.bfloat16
    )
    final_result = final_result.reshape(owner_count, taken_rows, final_result.shape[1])
    return lax.all_to_all(final_result, "batch", split_axis=0, concat_axis=0, tiled=True)


def body(
    queries,
    cached_keys,
    cached_values,
    token_key,
    token_value,
    lengths,
    adapter_index,
    output_weight,
    adapter_down,
    adapter_up,
):
    rows = queries.shape[0]
    width = queries.shape[1]
    span = cached_keys.shape[1]
    kv_local = cached_keys.shape[2] // HEAD_SIZE
    group = width // HEAD_SIZE // kv_local
    score_scale = HEAD_SIZE ** (-0.5)
    query_rows = queries.reshape(rows, kv_local, group, HEAD_SIZE)
    keys = cached_keys.reshape(rows, span, kv_local, HEAD_SIZE)
    values = cached_values.reshape(rows, span, kv_local, HEAD_SIZE)
    newest_key = token_key.reshape(rows, kv_local, HEAD_SIZE)
    fresh_value = token_value.reshape(rows, kv_local, HEAD_SIZE)
    scores = (
        jnp.einsum("rkgd,rlkd->rkgl", query_rows, keys, preferred_element_type=jnp.float32)
        * score_scale
    )
    owned_rows = (
        jnp.einsum("rkgd,rkd->rkg", query_rows, newest_key, preferred_element_type=jnp.float32)
        * score_scale
    )
    valid = lax.broadcasted_iota(jnp.int32, (rows, span), 1) < lengths[:, None]
    scores = jnp.where(valid[:, None, None, :], scores, -jnp.inf)
    top = jnp.maximum(jnp.max(scores, axis=-1), owned_rows)
    expo = jnp.exp(scores - top[..., None])
    own_expo = jnp.exp(owned_rows - top)
    total = jnp.sum(expo, axis=-1) + own_expo
    weights = (expo / total[..., None]).astype(jnp.bfloat16)
    own_weight = (own_expo / total).astype(jnp.bfloat16)
    mixed = jnp.einsum("rkgl,rlkd->rkgd", weights, values, preferred_element_type=jnp.float32)
    mixed = (
        mixed
        + own_weight.astype(jnp.float32)[..., None] * fresh_value.astype(jnp.float32)[:, :, None, :]
    )
    attention_output = mixed.reshape(rows, width).astype(jnp.bfloat16)
    owner_count = lax.axis_size("batch")
    held_rows = adapter_down.shape[0]
    slots = max(2, 2 * rows // owner_count)
    table = owner_count * slots
    partial_sums = jnp.dot(
        lax.all_gather(attention_output, "batch", axis=0, tiled=True),
        output_weight,
        preferred_element_type=jnp.float32,
    )
    routed = lax.all_to_all(partial_sums, "batch", split_axis=0, concat_axis=1, tiled=True)
    base_output = lax.psum_scatter(routed, "tensor", scatter_dimension=1, tiled=True)
    owner = adapter_index // held_rows
    local = adapter_index % held_rows
    owner_hot = (owner[:, None] == lax.broadcasted_iota(jnp.int32, (rows, owner_count), 1)).astype(
        jnp.bfloat16
    )
    earlier = (
        lax.broadcasted_iota(jnp.int32, (rows, rows), 0)
        > lax.broadcasted_iota(jnp.int32, (rows, rows), 1)
    ).astype(jnp.bfloat16)
    before = jnp.dot(earlier, owner_hot, preferred_element_type=jnp.float32)
    position = jnp.sum(before * owner_hot.astype(jnp.float32), axis=1).astype(jnp.int32)
    target = owner * slots + position
    place_rows = (target[:, None] == lax.broadcasted_iota(jnp.int32, (rows, table), 1)).astype(
        jnp.bfloat16
    )
    send_rows = jnp.einsum(
        "rs,rf->sf", place_rows, attention_output, preferred_element_type=jnp.float32
    ).astype(jnp.bfloat16)
    marked = jnp.where(place_rows > 0, (local[:, None] + 1).astype(jnp.float32), 0.0)
    send_ids = (jnp.max(marked, axis=0) - 1.0).astype(jnp.bfloat16)
    send_rows = send_rows.reshape(owner_count, slots, width)
    send_ids = send_ids.reshape(owner_count, slots)
    incoming = lax.all_to_all(send_rows, "batch", split_axis=0, concat_axis=0, tiled=True)
    tags = lax.all_to_all(send_ids, "batch", split_axis=0, concat_axis=0, tiled=True)
    taken_rows = incoming.shape[1]
    flattened_rows = incoming.reshape(-1, width)
    flat_tags = tags.reshape(-1).astype(jnp.float32)
    select_local = (
        flat_tags[:, None]
        == lax.broadcasted_iota(jnp.float32, (flattened_rows.shape[0], held_rows), 1)
    ).astype(jnp.float32)
    returned_output = finish_output(
        flattened_rows, select_local, adapter_down, adapter_up, owner_count, taken_rows
    )
    returned_output = returned_output.reshape(table, -1)
    adapter_rows = jnp.dot(place_rows, returned_output, preferred_element_type=jnp.float32)
    return (base_output + adapter_rows).astype(jnp.bfloat16)


F32 = jnp.float32
BF16 = jnp.bfloat16
PIECES = 3
STEP_ROWS = 16
LANES = 128


def remote(src, dst, send_sem, recv_sem, batch, tensor):
    return pltpu.make_async_remote_copy(
        src_ref=src,
        dst_ref=dst,
        send_sem=send_sem,
        recv_sem=recv_sem,
        device_id={"batch": batch, "tensor": tensor},
        device_id_type=pl.DeviceIdType.MESH,
    )


def attend_rows(r0, q_v, k_v, v_v, tk_ref, tv_ref, len_ref, attn_all, z):
    group = 8
    rows = group * STEP_ROWS
    span = 64
    pos_rows = pl.ds(pl.multiple_of(r0 * span, STEP_ROWS * span), STEP_ROWS * span)
    req = pl.ds(r0, STEP_ROWS)
    row = lax.broadcasted_iota(jnp.int32, (rows, LANES), 0)
    lane = lax.broadcasted_iota(jnp.int32, (rows, LANES), 1)
    in_step = row % STEP_ROWS
    pair = in_step // 2
    lens = jnp.concatenate([len_ref[req, :]] * group, axis=0)
    valid = ((in_step % 2) == (lane // span)) & ((lane % span) < lens)
    scale = HEAD_SIZE ** (-0.5)
    for kv in range(2):
        cols = slice(kv * HEAD_SIZE, (kv + 1) * HEAD_SIZE)
        q = jnp.concatenate(
            [
                q_v[req, (kv * group + h) * HEAD_SIZE : (kv * group + h + 1) * HEAD_SIZE]
                for h in range(group)
            ],
            axis=0,
        )
        s = lax.dot_general(
            q, k_v[pos_rows, cols], (((1,), (1,)), ((), ())), preferred_element_type=F32
        )
        c = s[:, :LANES]
        for j in range(1, STEP_ROWS // 2):
            c = jnp.where(pair == j, s[:, j * LANES : (j + 1) * LANES], c)
        c = jnp.where(valid, c * scale, -jnp.inf)
        tk = jnp.concatenate([tk_ref[req, cols].astype(F32)] * group, axis=0)
        own = jnp.sum(q.astype(F32) * tk, axis=1, keepdims=True) * scale
        top = jnp.maximum(jnp.max(c, axis=1, keepdims=True), own)
        e = jnp.exp(c - top)
        own_e = jnp.exp(own - top)
        total = jnp.sum(e, axis=1, keepdims=True) + own_e
        p = e / total
        own_w = (own_e / total).astype(BF16).astype(F32)
        wide = jnp.concatenate(
            [jnp.where(pair == j, p, 0.0).astype(BF16) for j in range(STEP_ROWS // 2)], axis=1
        )
        o = jnp.dot(wide, v_v[pos_rows, cols], preferred_element_type=F32)
        tv = jnp.concatenate([tv_ref[req, cols].astype(F32)] * group, axis=0)
        o = (o + own_w * tv).astype(BF16)
        for h in range(group):
            head = kv * group + h
            attn_all[z, req, head * HEAD_SIZE : (head + 1) * HEAD_SIZE] = o[
                h * STEP_ROWS : (h + 1) * STEP_ROWS
            ]


def placement(ids, owner, held, rows):
    low = (owner * held).astype(F32)
    mine = (ids >= low) & (ids < low + held)
    tri = (
        lax.broadcasted_iota(jnp.int32, (rows, rows), 0)
        > lax.broadcasted_iota(jnp.int32, (rows, rows), 1)
    )
    rank = jnp.dot(
        jnp.where(tri, 1.0, 0.0).astype(BF16),
        jnp.where(mine, 1.0, 0.0).astype(BF16),
        preferred_element_type=F32,
    )
    slot = lax.broadcasted_iota(jnp.int32, (rows, LANES), 1).astype(F32)
    return jnp.where(mine & (rank == slot), 1.0, 0.0).astype(BF16)


def kernel(
    q_hbm, k_hbm, v_hbm, tk_ref, tv_ref, len_ref, ids_ref, w_hbm, down_hbm, up_hbm,
    out_ref,
    q_v, k_v, v_v, w_v, down_v, up_v,
    ids_all, attn_all, u_send, u_recv, rs_send, rs_own, rs_recv,
    lora_send, lora_recv, out_send, out_recv,
    load_sem, id_ssem, id_rsem, at_ssem, fw_ssem, at_rsem, u_ssem, u_rsem,
    rs_ssem, rs_rsem, lo_ssem, lo_rsem, out_ssem, out_rsem,
):
    z = lax.axis_index("batch")
    t = lax.axis_index("tensor")
    rows, width = out_ref.shape
    n = 4
    held = down_v.shape[0]
    rank_width = down_v.shape[2]
    slots = lora_send.shape[1]
    quarter = width // n
    half = rows // 2
    piece = rows // PIECES
    span = k_v.shape[0] // rows

    barrier = pltpu.get_barrier_semaphore()
    for i in range(1, n * n):
        other = (z * n + t + i) % (n * n)
        pl.semaphore_signal(
            barrier,
            inc=1,
            device_id={"batch": other // n, "tensor": other % n},
            device_id_type=pl.DeviceIdType.MESH,
        )

    loads = [pltpu.make_async_copy(q_hbm, q_v, load_sem.at[0])]
    for p in range(PIECES):
        part = pl.ds(p * piece * span, piece * span)
        loads.append(pltpu.make_async_copy(k_hbm.at[part], k_v.at[part], load_sem.at[1 + 2 * p]))
        loads.append(pltpu.make_async_copy(v_hbm.at[part], v_v.at[part], load_sem.at[2 + 2 * p]))
    tail_loads = [
        pltpu.make_async_copy(down_hbm, down_v, load_sem.at[7]),
        pltpu.make_async_copy(w_hbm, w_v, load_sem.at[8]),
        pltpu.make_async_copy(up_hbm, up_v, load_sem.at[9]),
    ]
    for load in loads + tail_loads:
        load.start()
    ids_all[z] = ids_ref[...]

    def id_copy(i):
        return remote(ids_all.at[z], ids_all.at[z], id_ssem.at[i - 1], id_rsem.at[z], (z + i) % n, t)

    def own_copy(direction, p):
        part = attn_all.at[z, pl.ds(p * piece, piece)]
        to = z + 1 if direction else z - 1
        return remote(part, part, at_ssem.at[direction, p], at_rsem.at[z, p], to, t)

    loads[0].wait()
    for p in range(PIECES):
        loads[1 + 2 * p].wait()
        loads[2 + 2 * p].wait()

        def step(i, carry):
            r0 = pl.multiple_of(i * STEP_ROWS, STEP_ROWS)
            attend_rows(r0, q_v, k_v, v_v, tk_ref, tv_ref, len_ref, attn_all, z)
            return carry

        per = piece // STEP_ROWS
        lax.fori_loop(p * per, (p + 1) * per, step, 0)
        if p == 0:
            pl.semaphore_wait(barrier, n * n - 1)
            for i in range(1, n):
                id_copy(i).start()

        @pl.when(z < n - 1)
        def _():
            own_copy(1, p).start()

        @pl.when(z > 0)
        def _():
            own_copy(0, p).start()

    blocks = [z, z + 1 - 2 * (z % 2), 2 - z // 2, 3 - 3 * (z // 2)]

    def block_ids(b):
        return ids_all[b].astype(F32)

    def adapter_mask(ids, j):
        return ids[:, :rank_width] == (z * held + j).astype(F32)

    def forward(k, p, to):
        b = blocks[k]
        part = attn_all.at[b, pl.ds(p * piece, piece)]
        return remote(part, part, fw_ssem.at[k, p], at_rsem.at[b, p], to, t)

    def u_copy(k, i):
        return remote(
            u_send.at[k], u_recv.at[k, t], u_ssem.at[k, i - 1], u_rsem.at[k, t], z, (t + i) % n
        )

    def rs_copy(k, i):
        return remote(
            rs_send.at[k, i - 1], rs_recv.at[k, t], rs_ssem.at[k, i - 1], rs_rsem.at[k, t],
            z, (t + i) % n,
        )

    def lora_copy(k):
        return remote(
            lora_send.at[k], lora_recv.at[z], lo_ssem.at[k], lo_rsem.at[z], blocks[k], t
        )

    def out_copy(k):
        return remote(out_send.at[k], out_recv.at[t], out_ssem.at[k], out_rsem.at[t], blocks[k], z)

    middle = (z * (n - 1 - z)) > 0

    def relay_to(k):
        return z - 1 + 2 * (z % 2) if k == 1 else z - 1 + 2 * (z // 2)

    def main(k):
        b = blocks[k]
        if k > 0:
            for p in range(PIECES):
                forward(k, p, z).wait_recv()

                @pl.when(middle)
                def _():
                    forward(k, p, relay_to(k)).start()

            remote(ids_all.at[b], ids_all.at[b], id_ssem.at[0], id_rsem.at[b], z, t).wait_recv()
        x = attn_all[b]
        ids = block_ids(b)
        u = jnp.zeros((rows, rank_width), F32)
        for j in range(held):
            uj = jnp.dot(x, down_v[j], preferred_element_type=F32)
            u = jnp.where(adapter_mask(ids, j), uj, u)
        u_send[k] = jnp.concatenate([u[:half], u[half:]], axis=1)
        for i in range(1, n):
            u_copy(k, i).start()

        def project(i, carry):
            q = (t + i) % n
            cols = pl.ds(pl.multiple_of(q * quarter, quarter), quarter)
            part = jnp.dot(attn_all[b], w_v[:, cols], preferred_element_type=F32)
            rs_send[k, i - 1] = part.astype(BF16)
            rs_copy(k, i).start()
            return carry

        lax.fori_loop(1, n, project, 0)
        cols = pl.ds(pl.multiple_of(t * quarter, quarter), quarter)
        rs_own[k] = jnp.dot(attn_all[b], w_v[:, cols], preferred_element_type=F32)

    def post(k):
        b = blocks[k]
        total = u_send[k]
        for i in range(1, n):
            src = (t + i) % n
            remote(
                u_recv.at[k, src], u_recv.at[k, src], u_ssem.at[k, i - 1], u_rsem.at[k, src], z, src
            ).wait_recv()
            total = total + u_recv[k, src]
        u = jnp.concatenate([total[:, :rank_width], total[:, rank_width:]], axis=0)
        ids = block_ids(b)
        place = placement(ids, z, held, rows)
        compact = []
        for j in range(held):
            uj = jnp.where(adapter_mask(ids, j), u, 0.0).astype(BF16)
            cj = lax.dot_general(place, uj, (((0,), (0,)), ((), ())), preferred_element_type=F32)
            compact.append(cj[:slots].astype(BF16))
        target = lora_recv.at[z] if k == 0 else lora_send.at[k]
        for q in range(n):
            cs = slice(q * quarter, (q + 1) * quarter)
            acc = jnp.dot(compact[0], up_v[0, :, cs], preferred_element_type=F32)
            for j in range(1, held):
                acc = acc + jnp.dot(compact[j], up_v[j, :, cs], preferred_element_type=F32)
            target[:, cs] = (adapter_scale * acc).astype(BF16)
        if k > 0:
            lora_copy(k).start()

        sums = rs_own[k]
        for i in range(1, n):
            src = (t + i) % n
            remote(
                rs_recv.at[k, src], rs_recv.at[k, src], rs_ssem.at[k, i - 1], rs_rsem.at[k, src],
                z, src,
            ).wait_recv()
            sums = sums + rs_recv[k, src].astype(F32)
        out_send[k] = sums.astype(BF16)
        if k > 0:
            out_copy(k).start()
        else:

            @pl.when(t != z)
            def _():
                out_copy(0).start()

            @pl.when(t == z)
            def _():
                out_recv[t] = out_send[0]

    for load in tail_loads:
        load.wait()
    main(0)
    for k in range(1, n):
        main(k)
        post(k - 1)
    post(n - 1)

    ids = block_ids(z)
    places = [placement(ids, z * 0 + o, held, rows)[:, :slots] for o in range(n)]
    for k in range(1, n):
        b = blocks[k]
        remote(
            lora_recv.at[b], lora_recv.at[b], lo_ssem.at[k], lo_rsem.at[b], z, t
        ).wait_recv()
    for src in range(n):

        def arrive(src=src):
            remote(
                out_recv.at[src], out_recv.at[src], out_ssem.at[0], out_rsem.at[src], z, t
            ).wait_recv()

        pl.when((z - t) * (z - t) + (src - t) * (src - t) > 0)(arrive)
        cs = slice(src * quarter, (src + 1) * quarter)
        acc = out_recv[src].astype(F32)
        for o in range(n):
            acc = acc + jnp.dot(places[o], lora_recv[o, :, cs], preferred_element_type=F32)
        out_ref[:, cs] = acc.astype(BF16)

    for i in range(1, n):
        id_copy(i).wait_send()
    for p in range(PIECES):

        @pl.when(z < n - 1)
        def _():
            own_copy(1, p).wait_send()

        @pl.when(z > 0)
        def _():
            own_copy(0, p).wait_send()

        @pl.when(middle)
        def _():
            for k in range(1, n):
                forward(k, p, relay_to(k)).wait_send()

    for k in range(n):
        for i in range(1, n):
            u_copy(k, i).wait_send()
            rs_copy(k, i).wait_send()
        if k > 0:
            lora_copy(k).wait_send()
            out_copy(k).wait_send()
        else:

            @pl.when(t != z)
            def _():
                out_copy(0).wait_send()


def fused_body(
    queries, cached_keys, cached_values, token_key, token_value, lengths, adapter_index,
    output_weight, adapter_down, adapter_up,
):
    rows, width = queries.shape
    span, kv_width = cached_keys.shape[1:]
    n = lax.axis_size("batch")
    held, _, rank_width = adapter_down.shape
    slots = max(2, 2 * rows // n)
    quarter = width // n
    lens = jnp.broadcast_to(lengths[:, None], (rows, LANES))
    ids = jnp.broadcast_to(adapter_index[:, None], (rows, LANES)).astype(BF16)
    vmem = pl.BlockSpec(memory_space=pltpu.VMEM)
    hbm = pl.BlockSpec(memory_space=pl.ANY)
    dma = pltpu.SemaphoreType.DMA
    flops = 2 * rows * n * width * (width + held * rank_width)
    return pl.pallas_call(
        kernel,
        out_shape=jax.ShapeDtypeStruct((rows, width), BF16),
        in_specs=[hbm, hbm, hbm, vmem, vmem, vmem, vmem, hbm, hbm, hbm],
        out_specs=vmem,
        scratch_shapes=[
            pltpu.VMEM((rows, width), BF16),
            pltpu.VMEM((rows * span, kv_width), BF16),
            pltpu.VMEM((rows * span, kv_width), BF16),
            pltpu.VMEM(output_weight.shape, BF16),
            pltpu.VMEM(adapter_down.shape, BF16),
            pltpu.VMEM(adapter_up.shape, BF16),
            pltpu.VMEM((n, rows, LANES), BF16),
            pltpu.VMEM((n, rows, width), BF16),
            pltpu.VMEM((n, rows // 2, 2 * rank_width), F32),
            pltpu.VMEM((n, n, rows // 2, 2 * rank_width), F32),
            pltpu.VMEM((n, n - 1, rows, quarter), BF16),
            pltpu.VMEM((n, rows, quarter), F32),
            pltpu.VMEM((n, n, rows, quarter), BF16),
            pltpu.VMEM((n, slots, width), BF16),
            pltpu.VMEM((n, slots, width), BF16),
            pltpu.VMEM((n, rows, quarter), BF16),
            pltpu.VMEM((n, rows, quarter), BF16),
            dma((10,)),
            dma((n - 1,)), dma((n,)),
            dma((2, PIECES)), dma((n, PIECES)), dma((n, PIECES)),
            dma((n, n - 1)), dma((n, n)),
            dma((n, n - 1)), dma((n, n)),
            dma((n,)), dma((n,)),
            dma((n,)), dma((n,)),
        ],
        cost_estimate=pl.CostEstimate(
            flops=flops, bytes_accessed=2 * (width * width + 2 * rows * span * kv_width),
            transcendentals=0,
        ),
        compiler_params=pltpu.CompilerParams(
            collective_id=0, has_side_effects=True, vmem_limit_bytes=50 * 2**20
        ),
    )(
        queries,
        cached_keys.reshape(rows * span, kv_width),
        cached_values.reshape(rows * span, kv_width),
        token_key,
        token_value,
        lens,
        ids,
        output_weight,
        adapter_down,
        adapter_up,
    )


def solution(mesh):
    fused = mesh.shape["batch"] == 4 and mesh.shape["tensor"] == 4
    placed = (
        P(("groups", "batch"), "tensor"),
        P(("groups", "batch"), None, "tensor"),
        P(("groups", "batch"), None, "tensor"),
        P(("groups", "batch"), "tensor"),
        P(("groups", "batch"), "tensor"),
        P(("groups", "batch")),
        P(("groups", "batch")),
        P("tensor", "batch"),
        P("batch", "tensor", None),
        P("batch", None, "tensor"),
    )
    return jax.shard_map(
        fused_body if fused else body,
        mesh=mesh,
        in_specs=placed,
        out_specs=P(("groups", "batch"), "tensor"),
        check_vma=False,
    )
```

```python
import jax
import jax.numpy as jnp
from jax import lax
from jax.experimental import pallas as pl
from jax.experimental.pallas import tpu as pltpu
from jax.sharding import PartitionSpec as P

HEAD_SIZE = 128


adapter_scale = 0.25


def finish_output(
    flattened_rows, select_adapter, adapter_down, adapter_up, owner_count, taken_rows
):
    down_factor = jnp.einsum(
        "tj,ojx->tox", flattened_rows, adapter_down, preferred_element_type=jnp.float32
    )
    partial_small = jnp.einsum("sak,sa->sk", down_factor, select_adapter)
    small_product = lax.psum(partial_small, "tensor").astype(jnp.bfloat16)
    up_factor = jnp.einsum(
        "yg,rgo->yro", small_product, adapter_up, preferred_element_type=jnp.float32
    )
    final_result = (adapter_scale * jnp.einsum("czp,cz->cp", up_factor, select_adapter)).astype(
        jnp.bfloat16
    )
    final_result = final_result.reshape(owner_count, taken_rows, final_result.shape[1])
    return lax.all_to_all(final_result, "batch", split_axis=0, concat_axis=0, tiled=True)


def body(
    queries,
    cached_keys,
    cached_values,
    token_key,
    token_value,
    lengths,
    adapter_index,
    output_weight,
    adapter_down,
    adapter_up,
):
    rows = queries.shape[0]
    width = queries.shape[1]
    span = cached_keys.shape[1]
    kv_local = cached_keys.shape[2] // HEAD_SIZE
    group = width // HEAD_SIZE // kv_local
    score_scale = HEAD_SIZE ** (-0.5)
    query_rows = queries.reshape(rows, kv_local, group, HEAD_SIZE)
    keys = cached_keys.reshape(rows, span, kv_local, HEAD_SIZE)
    values = cached_values.reshape(rows, span, kv_local, HEAD_SIZE)
    newest_key = token_key.reshape(rows, kv_local, HEAD_SIZE)
    fresh_value = token_value.reshape(rows, kv_local, HEAD_SIZE)
    scores = (
        jnp.einsum("rkgd,rlkd->rkgl", query_rows, keys, preferred_element_type=jnp.float32)
        * score_scale
    )
    owned_rows = (
        jnp.einsum("rkgd,rkd->rkg", query_rows, newest_key, preferred_element_type=jnp.float32)
        * score_scale
    )
    valid = lax.broadcasted_iota(jnp.int32, (rows, span), 1) < lengths[:, None]
    scores = jnp.where(valid[:, None, None, :], scores, -jnp.inf)
    top = jnp.maximum(jnp.max(scores, axis=-1), owned_rows)
    expo = jnp.exp(scores - top[..., None])
    own_expo = jnp.exp(owned_rows - top)
    total = jnp.sum(expo, axis=-1) + own_expo
    weights = (expo / total[..., None]).astype(jnp.bfloat16)
    own_weight = (own_expo / total).astype(jnp.bfloat16)
    mixed = jnp.einsum("rkgl,rlkd->rkgd", weights, values, preferred_element_type=jnp.float32)
    mixed = (
        mixed
        + own_weight.astype(jnp.float32)[..., None] * fresh_value.astype(jnp.float32)[:, :, None, :]
    )
    attention_output = mixed.reshape(rows, width).astype(jnp.bfloat16)
    owner_count = lax.axis_size("batch")
    held_rows = adapter_down.shape[0]
    slots = max(2, 2 * rows // owner_count)
    table = owner_count * slots
    partial_sums = jnp.dot(
        lax.all_gather(attention_output, "batch", axis=0, tiled=True),
        output_weight,
        preferred_element_type=jnp.float32,
    )
    routed = lax.all_to_all(partial_sums, "batch", split_axis=0, concat_axis=1, tiled=True)
    base_output = lax.psum_scatter(routed, "tensor", scatter_dimension=1, tiled=True)
    owner = adapter_index // held_rows
    local = adapter_index % held_rows
    owner_hot = (owner[:, None] == lax.broadcasted_iota(jnp.int32, (rows, owner_count), 1)).astype(
        jnp.bfloat16
    )
    earlier = (
        lax.broadcasted_iota(jnp.int32, (rows, rows), 0)
        > lax.broadcasted_iota(jnp.int32, (rows, rows), 1)
    ).astype(jnp.bfloat16)
    before = jnp.dot(earlier, owner_hot, preferred_element_type=jnp.float32)
    position = jnp.sum(before * owner_hot.astype(jnp.float32), axis=1).astype(jnp.int32)
    target = owner * slots + position
    place_rows = (target[:, None] == lax.broadcasted_iota(jnp.int32, (rows, table), 1)).astype(
        jnp.bfloat16
    )
    send_rows = jnp.einsum(
        "rs,rf->sf", place_rows, attention_output, preferred_element_type=jnp.float32
    ).astype(jnp.bfloat16)
    marked = jnp.where(place_rows > 0, (local[:, None] + 1).astype(jnp.float32), 0.0)
    send_ids = (jnp.max(marked, axis=0) - 1.0).astype(jnp.bfloat16)
    send_rows = send_rows.reshape(owner_count, slots, width)
    send_ids = send_ids.reshape(owner_count, slots)
    incoming = lax.all_to_all(send_rows, "batch", split_axis=0, concat_axis=0, tiled=True)
    tags = lax.all_to_all(send_ids, "batch", split_axis=0, concat_axis=0, tiled=True)
    taken_rows = incoming.shape[1]
    flattened_rows = incoming.reshape(-1, width)
    flat_tags = tags.reshape(-1).astype(jnp.float32)
    select_local = (
        flat_tags[:, None]
        == lax.broadcasted_iota(jnp.float32, (flattened_rows.shape[0], held_rows), 1)
    ).astype(jnp.float32)
    returned_output = finish_output(
        flattened_rows, select_local, adapter_down, adapter_up, owner_count, taken_rows
    )
    returned_output = returned_output.reshape(table, -1)
    adapter_rows = jnp.dot(place_rows, returned_output, preferred_element_type=jnp.float32)
    return (base_output + adapter_rows).astype(jnp.bfloat16)


F32 = jnp.float32
BF16 = jnp.bfloat16
PIECES = 3
STEP_ROWS = 16
LANES = 128


def remote(src, dst, send_sem, recv_sem, batch, tensor):
    return pltpu.make_async_remote_copy(
        src_ref=src,
        dst_ref=dst,
        send_sem=send_sem,
        recv_sem=recv_sem,
        device_id={"batch": batch, "tensor": tensor},
        device_id_type=pl.DeviceIdType.MESH,
    )


def attend_rows(r0, q_v, k_v, v_v, tk_ref, tv_ref, len_ref, attn_all, z):
    group = 8
    rows = group * STEP_ROWS
    span = 64
    pos_rows = pl.ds(pl.multiple_of(r0 * span, STEP_ROWS * span), STEP_ROWS * span)
    req = pl.ds(r0, STEP_ROWS)
    row = lax.broadcasted_iota(jnp.int32, (rows, LANES), 0)
    lane = lax.broadcasted_iota(jnp.int32, (rows, LANES), 1)
    in_step = row % STEP_ROWS
    pair = in_step // 2
    lens = jnp.concatenate([len_ref[req, :]] * group, axis=0)
    valid = ((in_step % 2) == (lane // span)) & ((lane % span).astype(F32) < lens)
    scale = HEAD_SIZE ** (-0.5)
    for kv in range(2):
        cols = slice(kv * HEAD_SIZE, (kv + 1) * HEAD_SIZE)
        q = jnp.concatenate(
            [
                q_v[req, (kv * group + h) * HEAD_SIZE : (kv * group + h + 1) * HEAD_SIZE]
                for h in range(group)
            ],
            axis=0,
        )
        s = lax.dot_general(
            q, k_v[pos_rows, cols], (((1,), (1,)), ((), ())), preferred_element_type=F32
        )
        c = s[:, :LANES]
        for j in range(1, STEP_ROWS // 2):
            c = jnp.where(pair == j, s[:, j * LANES : (j + 1) * LANES], c)
        c = jnp.where(valid, c * scale, -jnp.inf)
        tk = jnp.concatenate([tk_ref[req, cols].astype(F32)] * group, axis=0)
        own = jnp.sum(q.astype(F32) * tk, axis=1, keepdims=True) * scale
        top = jnp.maximum(jnp.max(c, axis=1, keepdims=True), own)
        e = jnp.exp(c - top)
        own_e = jnp.exp(own - top)
        total = jnp.sum(e, axis=1, keepdims=True) + own_e
        p = e / total
        own_w = (own_e / total).astype(BF16).astype(F32)
        wide = jnp.concatenate(
            [jnp.where(pair == j, p, 0.0).astype(BF16) for j in range(STEP_ROWS // 2)], axis=1
        )
        o = jnp.dot(wide, v_v[pos_rows, cols], preferred_element_type=F32)
        tv = jnp.concatenate([tv_ref[req, cols].astype(F32)] * group, axis=0)
        o = (o + own_w * tv).astype(BF16)
        for h in range(group):
            head = kv * group + h
            attn_all[z, req, head * HEAD_SIZE : (head + 1) * HEAD_SIZE] = o[
                h * STEP_ROWS : (h + 1) * STEP_ROWS
            ]


def placement(ids, owner, held, rows):
    low = (owner * held).astype(F32)
    mine = (ids >= low) & (ids < low + held)
    tri = (
        lax.broadcasted_iota(jnp.int32, (rows, rows), 0)
        > lax.broadcasted_iota(jnp.int32, (rows, rows), 1)
    )
    rank = jnp.dot(
        jnp.where(tri, 1.0, 0.0).astype(BF16),
        jnp.where(mine, 1.0, 0.0).astype(BF16),
        preferred_element_type=F32,
    )
    slot = lax.broadcasted_iota(jnp.int32, (rows, LANES), 1).astype(F32)
    return jnp.where(mine & (rank == slot), 1.0, 0.0).astype(BF16)


def kernel(
    q_hbm, k_hbm, v_hbm, tk_hbm, tv_hbm, len_hbm, ids_hbm, w_hbm, down_hbm, up_hbm,
    out_ref,
    q_v, k_v, v_v, w_v, down_v, up_v, tk_ref, tv_ref, len_v, ids_v, len_ref,
    ids_all, attn_all, u_send, u_recv, rs_send, rs_own, rs_recv,
    lora_send, lora_recv, out_send, out_recv,
    load_sem, id_ssem, id_rsem, at_ssem, fw_ssem, at_rsem, u_ssem, u_rsem,
    rs_ssem, rs_rsem, lo_ssem, lo_rsem, out_ssem, out_rsem,
):
    z = lax.axis_index("batch")
    t = lax.axis_index("tensor")
    rows, width = out_ref.shape
    n = 4
    held = down_v.shape[0]
    rank_width = down_v.shape[1]
    slots = lora_send.shape[1]
    quarter = width // n
    half = rows // 2
    piece = rows // PIECES
    span = k_v.shape[0] // rows

    barrier = pltpu.get_barrier_semaphore()
    for i in range(1, n * n):
        other = (z * n + t + i) % (n * n)
        pl.semaphore_signal(
            barrier,
            inc=1,
            device_id={"batch": other // n, "tensor": other % n},
            device_id_type=pl.DeviceIdType.MESH,
        )

    small_loads = [
        pltpu.make_async_copy(len_hbm, len_v, load_sem.at[10]),
        pltpu.make_async_copy(ids_hbm, ids_v, load_sem.at[11]),
        pltpu.make_async_copy(tk_hbm, tk_ref, load_sem.at[12]),
        pltpu.make_async_copy(tv_hbm, tv_ref, load_sem.at[13]),
    ]
    loads = [pltpu.make_async_copy(q_hbm, q_v, load_sem.at[0])]
    for p in range(PIECES):
        part = pl.ds(p * piece * span, piece * span)
        loads.append(pltpu.make_async_copy(k_hbm.at[part], k_v.at[part], load_sem.at[1 + 2 * p]))
        loads.append(pltpu.make_async_copy(v_hbm.at[part], v_v.at[part], load_sem.at[2 + 2 * p]))
    tail_loads = [
        pltpu.make_async_copy(down_hbm, down_v, load_sem.at[7]),
        pltpu.make_async_copy(w_hbm, w_v, load_sem.at[8]),
        pltpu.make_async_copy(up_hbm, up_v, load_sem.at[9]),
    ]
    for load in small_loads + loads:
        load.start()
    for load in small_loads:
        load.wait()

    def by_row(line):
        return jnp.transpose(jnp.broadcast_to(line.astype(F32), (LANES, rows)))

    len_ref[...] = by_row(len_v[...])
    ids_all[z] = by_row(ids_v[...]).astype(BF16)

    def id_copy(i):
        return remote(ids_all.at[z], ids_all.at[z], id_ssem.at[i - 1], id_rsem.at[z], (z + i) % n, t)

    def own_copy(direction, p):
        part = attn_all.at[z, pl.ds(p * piece, piece)]
        to = z + 1 if direction else z - 1
        return remote(part, part, at_ssem.at[direction, p], at_rsem.at[z, p], to, t)

    loads[0].wait()
    for p in range(PIECES):
        loads[1 + 2 * p].wait()
        loads[2 + 2 * p].wait()
        if p == 0:
            for load in tail_loads:
                load.start()

        def step(i, carry):
            r0 = pl.multiple_of(i * STEP_ROWS, STEP_ROWS)
            attend_rows(r0, q_v, k_v, v_v, tk_ref, tv_ref, len_ref, attn_all, z)
            return carry

        per = piece // STEP_ROWS
        lax.fori_loop(p * per, (p + 1) * per, step, 0)
        if p == 0:
            pl.semaphore_wait(barrier, n * n - 1)
            for i in range(1, n):
                id_copy(i).start()

        @pl.when(z < n - 1)
        def _():
            own_copy(1, p).start()

        @pl.when(z > 0)
        def _():
            own_copy(0, p).start()

    blocks = [z, z + 1 - 2 * (z % 2), 2 - z // 2, 3 - 3 * (z // 2)]

    def block_ids(b):
        return ids_all[b].astype(F32)

    def adapter_mask(ids, j):
        return ids[:, :rank_width] == (z * held + j).astype(F32)

    def forward(k, p, to):
        b = blocks[k]
        part = attn_all.at[b, pl.ds(p * piece, piece)]
        return remote(part, part, fw_ssem.at[k, p], at_rsem.at[b, p], to, t)

    def u_copy(k, i):
        return remote(
            u_send.at[k], u_recv.at[k, t], u_ssem.at[k, i - 1], u_rsem.at[k, t], z, (t + i) % n
        )

    def rs_copy(k, i):
        return remote(
            rs_send.at[k, i - 1], rs_recv.at[k, t], rs_ssem.at[k, i - 1], rs_rsem.at[k, t],
            z, (t + i) % n,
        )

    def lora_copy(k):
        return remote(
            lora_send.at[k], lora_recv.at[z], lo_ssem.at[k], lo_rsem.at[z], blocks[k], t
        )

    def out_copy(k):
        return remote(out_send.at[k], out_recv.at[t], out_ssem.at[k], out_rsem.at[t], blocks[k], z)

    middle = (z * (n - 1 - z)) > 0

    def relay_to(k):
        return z - 1 + 2 * (z % 2) if k == 1 else z - 1 + 2 * (z // 2)

    def relay(k, pieces):
        @pl.when(middle)
        def _():
            for p in pieces:
                forward(k, p, z).wait_recv()
                forward(k, p, relay_to(k)).start()

    def main(k):
        b = blocks[k]
        if k > 0:
            @pl.when(jnp.logical_not(middle))
            def _():
                for p in range(PIECES):
                    forward(k, p, z).wait_recv()

            remote(ids_all.at[b], ids_all.at[b], id_ssem.at[0], id_rsem.at[b], z, t).wait_recv()
        x = attn_all[b]
        ids = block_ids(b)
        u = jnp.zeros((rows, rank_width), F32)
        for j in range(held):
            uj = lax.dot_general(
                x, down_v[j], (((1,), (1,)), ((), ())), preferred_element_type=F32
            )
            u = jnp.where(adapter_mask(ids, j), uj, u)
        u_send[k] = jnp.concatenate([u[:half], u[half:]], axis=1)
        for i in range(1, n):
            u_copy(k, i).start()

        def project(i, carry):
            q = (t + i) % n
            cols = pl.ds(pl.multiple_of(q * quarter, quarter), quarter)
            part = jnp.dot(attn_all[b], w_v[:, cols], preferred_element_type=F32)
            rs_send[k, i - 1] = part.astype(BF16)
            rs_copy(k, i).start()
            return carry

        lax.fori_loop(1, n, project, 0)
        cols = pl.ds(pl.multiple_of(t * quarter, quarter), quarter)
        rs_own[k] = jnp.dot(attn_all[b], w_v[:, cols], preferred_element_type=F32)

    def post(k):
        b = blocks[k]
        total = u_send[k]
        for i in range(1, n):
            src = (t + i) % n
            remote(
                u_recv.at[k, src], u_recv.at[k, src], u_ssem.at[k, i - 1], u_rsem.at[k, src], z, src
            ).wait_recv()
            total = total + u_recv[k, src]
        u = jnp.concatenate([total[:, :rank_width], total[:, rank_width:]], axis=0)
        ids = block_ids(b)
        place = placement(ids, z, held, rows)
        compact = []
        for j in range(held):
            uj = jnp.where(adapter_mask(ids, j), u, 0.0).astype(BF16)
            cj = lax.dot_general(place, uj, (((0,), (0,)), ((), ())), preferred_element_type=F32)
            compact.append(cj[:slots].astype(BF16))
        target = lora_recv.at[z] if k == 0 else lora_send.at[k]
        for q in range(n):
            cs = slice(q * quarter, (q + 1) * quarter)
            acc = jnp.dot(compact[0], up_v[0, :, cs], preferred_element_type=F32)
            for j in range(1, held):
                acc = acc + jnp.dot(compact[j], up_v[j, :, cs], preferred_element_type=F32)
            target[:, cs] = (adapter_scale * acc).astype(BF16)
        if k > 0:
            lora_copy(k).start()

        sums = rs_own[k]
        for i in range(1, n):
            src = (t + i) % n
            remote(
                rs_recv.at[k, src], rs_recv.at[k, src], rs_ssem.at[k, i - 1], rs_rsem.at[k, src],
                z, src,
            ).wait_recv()
            sums = sums + rs_recv[k, src].astype(F32)
        out_send[k] = sums.astype(BF16)
        if k > 0:
            out_copy(k).start()
        else:

            @pl.when(t != z)
            def _():
                out_copy(0).start()

            @pl.when(t == z)
            def _():
                out_recv[t] = out_send[0]

    for load in tail_loads:
        load.wait()
    main(0)
    for p in range(PIECES):
        relay(1, [p])
        relay(2, [p])
    main(1)
    relay(3, [0])
    post(0)
    relay(3, range(1, PIECES))
    main(2)
    post(1)
    main(3)
    post(2)
    post(3)

    ids = block_ids(z)
    places = [placement(ids, z * 0 + o, held, rows)[:, :slots] for o in range(n)]
    for k in range(1, n):
        b = blocks[k]
        remote(
            lora_recv.at[b], lora_recv.at[b], lo_ssem.at[k], lo_rsem.at[b], z, t
        ).wait_recv()
    for src in range(n):

        def arrive(src=src):
            remote(
                out_recv.at[src], out_recv.at[src], out_ssem.at[0], out_rsem.at[src], z, t
            ).wait_recv()

        pl.when((z - t) * (z - t) + (src - t) * (src - t) > 0)(arrive)
        cs = slice(src * quarter, (src + 1) * quarter)
        acc = out_recv[src].astype(F32)
        for o in range(n):
            acc = acc + jnp.dot(places[o], lora_recv[o, :, cs], preferred_element_type=F32)
        out_ref[:, cs] = acc.astype(BF16)

    for i in range(1, n):
        id_copy(i).wait_send()
    for p in range(PIECES):

        @pl.when(z < n - 1)
        def _():
            own_copy(1, p).wait_send()

        @pl.when(z > 0)
        def _():
            own_copy(0, p).wait_send()

        @pl.when(middle)
        def _():
            for k in range(1, n):
                forward(k, p, relay_to(k)).wait_send()

    for k in range(n):
        for i in range(1, n):
            u_copy(k, i).wait_send()
            rs_copy(k, i).wait_send()
        if k > 0:
            lora_copy(k).wait_send()
            out_copy(k).wait_send()
        else:

            @pl.when(t != z)
            def _():
                out_copy(0).wait_send()


def fused_body(
    queries, cached_keys, cached_values, token_key, token_value, lengths, adapter_index,
    output_weight, adapter_down, adapter_up,
):
    rows, width = queries.shape
    span, kv_width = cached_keys.shape[1:]
    n = lax.axis_size("batch")
    held, _, rank_width = adapter_down.shape
    slots = max(2, 2 * rows // n)
    quarter = width // n
    vmem = pl.BlockSpec(memory_space=pltpu.VMEM)
    hbm = pl.BlockSpec(memory_space=pl.ANY)
    dma = pltpu.SemaphoreType.DMA
    flops = 2 * rows * n * width * (width + held * rank_width)
    return pl.pallas_call(
        kernel,
        out_shape=jax.ShapeDtypeStruct((rows, width), BF16),
        in_specs=[hbm] * 10,
        out_specs=vmem,
        scratch_shapes=[
            pltpu.VMEM((rows, width), BF16),
            pltpu.VMEM((rows * span, kv_width), BF16),
            pltpu.VMEM((rows * span, kv_width), BF16),
            pltpu.VMEM(output_weight.shape, BF16),
            pltpu.VMEM((held, rank_width, width), BF16),
            pltpu.VMEM(adapter_up.shape, BF16),
            pltpu.VMEM(token_key.shape, BF16),
            pltpu.VMEM(token_value.shape, BF16),
            pltpu.VMEM((1, rows), jnp.int32),
            pltpu.VMEM((1, rows), jnp.int32),
            pltpu.VMEM((rows, LANES), F32),
            pltpu.VMEM((n, rows, LANES), BF16),
            pltpu.VMEM((n, rows, width), BF16),
            pltpu.VMEM((n, rows // 2, 2 * rank_width), F32),
            pltpu.VMEM((n, n, rows // 2, 2 * rank_width), F32),
            pltpu.VMEM((n, n - 1, rows, quarter), BF16),
            pltpu.VMEM((n, rows, quarter), F32),
            pltpu.VMEM((n, n, rows, quarter), BF16),
            pltpu.VMEM((n, slots, width), BF16),
            pltpu.VMEM((n, slots, width), BF16),
            pltpu.VMEM((n, rows, quarter), BF16),
            pltpu.VMEM((n, rows, quarter), BF16),
            dma((14,)),
            dma((n - 1,)), dma((n,)),
            dma((2, PIECES)), dma((n, PIECES)), dma((n, PIECES)),
            dma((n, n - 1)), dma((n, n)),
            dma((n, n - 1)), dma((n, n)),
            dma((n,)), dma((n,)),
            dma((n,)), dma((n,)),
        ],
        cost_estimate=pl.CostEstimate(
            flops=flops, bytes_accessed=2 * (width * width + 2 * rows * span * kv_width),
            transcendentals=0,
        ),
        compiler_params=pltpu.CompilerParams(
            collective_id=0, has_side_effects=True, vmem_limit_bytes=62 * 2**20
        ),
    )(
        queries,
        cached_keys.reshape(rows * span, kv_width),
        cached_values.reshape(rows * span, kv_width),
        token_key,
        token_value,
        lengths.reshape(1, rows),
        adapter_index.reshape(1, rows),
        output_weight,
        adapter_down.transpose(0, 2, 1),
        adapter_up,
    )


def solution(mesh):
    fused = mesh.shape["batch"] == 4 and mesh.shape["tensor"] == 4
    placed = (
        P(("groups", "batch"), "tensor"),
        P(("groups", "batch"), None, "tensor"),
        P(("groups", "batch"), None, "tensor"),
        P(("groups", "batch"), "tensor"),
        P(("groups", "batch"), "tensor"),
        P(("groups", "batch")),
        P(("groups", "batch")),
        P("tensor", "batch"),
        P("batch", "tensor", None),
        P("batch", None, "tensor"),
    )
    return jax.shard_map(
        fused_body if fused else body,
        mesh=mesh,
        in_specs=placed,
        out_specs=P(("groups", "batch"), "tensor"),
        check_vma=False,
    )
```

```python
import jax
import jax.numpy as jnp
from jax import lax
from jax.experimental import pallas as pl
from jax.experimental.pallas import tpu as pltpu
from jax.sharding import PartitionSpec as P

HEAD_SIZE = 128


adapter_scale = 0.25


def finish_output(
    flattened_rows, select_adapter, adapter_down, adapter_up, owner_count, taken_rows
):
    down_factor = jnp.einsum(
        "tj,ojx->tox", flattened_rows, adapter_down, preferred_element_type=jnp.float32
    )
    partial_small = jnp.einsum("sak,sa->sk", down_factor, select_adapter)
    small_product = lax.psum(partial_small, "tensor").astype(jnp.bfloat16)
    up_factor = jnp.einsum(
        "yg,rgo->yro", small_product, adapter_up, preferred_element_type=jnp.float32
    )
    final_result = (adapter_scale * jnp.einsum("czp,cz->cp", up_factor, select_adapter)).astype(
        jnp.bfloat16
    )
    final_result = final_result.reshape(owner_count, taken_rows, final_result.shape[1])
    return lax.all_to_all(final_result, "batch", split_axis=0, concat_axis=0, tiled=True)


def body(
    queries,
    cached_keys,
    cached_values,
    token_key,
    token_value,
    lengths,
    adapter_index,
    output_weight,
    adapter_down,
    adapter_up,
):
    rows = queries.shape[0]
    width = queries.shape[1]
    span = cached_keys.shape[1]
    kv_local = cached_keys.shape[2] // HEAD_SIZE
    group = width // HEAD_SIZE // kv_local
    score_scale = HEAD_SIZE ** (-0.5)
    query_rows = queries.reshape(rows, kv_local, group, HEAD_SIZE)
    keys = cached_keys.reshape(rows, span, kv_local, HEAD_SIZE)
    values = cached_values.reshape(rows, span, kv_local, HEAD_SIZE)
    newest_key = token_key.reshape(rows, kv_local, HEAD_SIZE)
    fresh_value = token_value.reshape(rows, kv_local, HEAD_SIZE)
    scores = (
        jnp.einsum("rkgd,rlkd->rkgl", query_rows, keys, preferred_element_type=jnp.float32)
        * score_scale
    )
    owned_rows = (
        jnp.einsum("rkgd,rkd->rkg", query_rows, newest_key, preferred_element_type=jnp.float32)
        * score_scale
    )
    valid = lax.broadcasted_iota(jnp.int32, (rows, span), 1) < lengths[:, None]
    scores = jnp.where(valid[:, None, None, :], scores, -jnp.inf)
    top = jnp.maximum(jnp.max(scores, axis=-1), owned_rows)
    expo = jnp.exp(scores - top[..., None])
    own_expo = jnp.exp(owned_rows - top)
    total = jnp.sum(expo, axis=-1) + own_expo
    weights = (expo / total[..., None]).astype(jnp.bfloat16)
    own_weight = (own_expo / total).astype(jnp.bfloat16)
    mixed = jnp.einsum("rkgl,rlkd->rkgd", weights, values, preferred_element_type=jnp.float32)
    mixed = (
        mixed
        + own_weight.astype(jnp.float32)[..., None] * fresh_value.astype(jnp.float32)[:, :, None, :]
    )
    attention_output = mixed.reshape(rows, width).astype(jnp.bfloat16)
    owner_count = lax.axis_size("batch")
    held_rows = adapter_down.shape[0]
    slots = max(2, 2 * rows // owner_count)
    table = owner_count * slots
    partial_sums = jnp.dot(
        lax.all_gather(attention_output, "batch", axis=0, tiled=True),
        output_weight,
        preferred_element_type=jnp.float32,
    )
    routed = lax.all_to_all(partial_sums, "batch", split_axis=0, concat_axis=1, tiled=True)
    base_output = lax.psum_scatter(routed, "tensor", scatter_dimension=1, tiled=True)
    owner = adapter_index // held_rows
    local = adapter_index % held_rows
    owner_hot = (owner[:, None] == lax.broadcasted_iota(jnp.int32, (rows, owner_count), 1)).astype(
        jnp.bfloat16
    )
    earlier = (
        lax.broadcasted_iota(jnp.int32, (rows, rows), 0)
        > lax.broadcasted_iota(jnp.int32, (rows, rows), 1)
    ).astype(jnp.bfloat16)
    before = jnp.dot(earlier, owner_hot, preferred_element_type=jnp.float32)
    position = jnp.sum(before * owner_hot.astype(jnp.float32), axis=1).astype(jnp.int32)
    target = owner * slots + position
    place_rows = (target[:, None] == lax.broadcasted_iota(jnp.int32, (rows, table), 1)).astype(
        jnp.bfloat16
    )
    send_rows = jnp.einsum(
        "rs,rf->sf", place_rows, attention_output, preferred_element_type=jnp.float32
    ).astype(jnp.bfloat16)
    marked = jnp.where(place_rows > 0, (local[:, None] + 1).astype(jnp.float32), 0.0)
    send_ids = (jnp.max(marked, axis=0) - 1.0).astype(jnp.bfloat16)
    send_rows = send_rows.reshape(owner_count, slots, width)
    send_ids = send_ids.reshape(owner_count, slots)
    incoming = lax.all_to_all(send_rows, "batch", split_axis=0, concat_axis=0, tiled=True)
    tags = lax.all_to_all(send_ids, "batch", split_axis=0, concat_axis=0, tiled=True)
    taken_rows = incoming.shape[1]
    flattened_rows = incoming.reshape(-1, width)
    flat_tags = tags.reshape(-1).astype(jnp.float32)
    select_local = (
        flat_tags[:, None]
        == lax.broadcasted_iota(jnp.float32, (flattened_rows.shape[0], held_rows), 1)
    ).astype(jnp.float32)
    returned_output = finish_output(
        flattened_rows, select_local, adapter_down, adapter_up, owner_count, taken_rows
    )
    returned_output = returned_output.reshape(table, -1)
    adapter_rows = jnp.dot(place_rows, returned_output, preferred_element_type=jnp.float32)
    return (base_output + adapter_rows).astype(jnp.bfloat16)


F32 = jnp.float32
BF16 = jnp.bfloat16
PIECES = 6
STEP_ROWS = 16
LANES = 128


def remote(src, dst, send_sem, recv_sem, batch, tensor):
    return pltpu.make_async_remote_copy(
        src_ref=src,
        dst_ref=dst,
        send_sem=send_sem,
        recv_sem=recv_sem,
        device_id={"batch": batch, "tensor": tensor},
        device_id_type=pl.DeviceIdType.MESH,
    )


def attend_rows(r0, q_v, k_v, v_v, tk_ref, tv_ref, len_ref, attn_all, z):
    group = 8
    rows = group * STEP_ROWS
    span = 64
    pos_rows = pl.ds(pl.multiple_of(r0 * span, STEP_ROWS * span), STEP_ROWS * span)
    req = pl.ds(r0, STEP_ROWS)
    row = lax.broadcasted_iota(jnp.int32, (rows, LANES), 0)
    lane = lax.broadcasted_iota(jnp.int32, (rows, LANES), 1)
    in_step = row % STEP_ROWS
    pair = in_step // 2
    lens = jnp.concatenate([len_ref[req, :]] * group, axis=0)
    valid = ((in_step % 2) == (lane // span)) & ((lane % span).astype(F32) < lens)
    scale = HEAD_SIZE ** (-0.5)
    for kv in range(2):
        cols = slice(kv * HEAD_SIZE, (kv + 1) * HEAD_SIZE)
        q = jnp.concatenate(
            [
                q_v[req, (kv * group + h) * HEAD_SIZE : (kv * group + h + 1) * HEAD_SIZE]
                for h in range(group)
            ],
            axis=0,
        )
        s = lax.dot_general(
            q, k_v[pos_rows, cols], (((1,), (1,)), ((), ())), preferred_element_type=F32
        )
        c = s[:, :LANES]
        for j in range(1, STEP_ROWS // 2):
            c = jnp.where(pair == j, s[:, j * LANES : (j + 1) * LANES], c)
        c = jnp.where(valid, c * scale, -jnp.inf)
        tk = jnp.concatenate([tk_ref[req, cols].astype(F32)] * group, axis=0)
        own = jnp.sum(q.astype(F32) * tk, axis=1, keepdims=True) * scale
        top = jnp.maximum(jnp.max(c, axis=1, keepdims=True), own)
        e = jnp.exp(c - top)
        own_e = jnp.exp(own - top)
        total = jnp.sum(e, axis=1, keepdims=True) + own_e
        p = e / total
        own_w = (own_e / total).astype(BF16).astype(F32)
        wide = jnp.concatenate(
            [jnp.where(pair == j, p, 0.0).astype(BF16) for j in range(STEP_ROWS // 2)], axis=1
        )
        o = jnp.dot(wide, v_v[pos_rows, cols], preferred_element_type=F32)
        tv = jnp.concatenate([tv_ref[req, cols].astype(F32)] * group, axis=0)
        o = (o + own_w * tv).astype(BF16)
        for h in range(group):
            head = kv * group + h
            attn_all[z, req, head * HEAD_SIZE : (head + 1) * HEAD_SIZE] = o[
                h * STEP_ROWS : (h + 1) * STEP_ROWS
            ]


def owner_ranks(ids, owner, held, rows):
    low = (owner * held).astype(F32)
    mine = (ids >= low) & (ids < low + held)
    tri = (
        lax.broadcasted_iota(jnp.int32, (rows, rows), 0)
        > lax.broadcasted_iota(jnp.int32, (rows, rows), 1)
    )
    rank = jnp.dot(
        jnp.where(tri, 1.0, 0.0).astype(BF16),
        jnp.where(mine, 1.0, 0.0).astype(BF16),
        preferred_element_type=F32,
    )
    return mine, rank


def kernel(
    q_hbm, k_hbm, v_hbm, tk_hbm, tv_hbm, len_hbm, ids_hbm, w_hbm, down_hbm, up_hbm,
    out_ref,
    q_v, k_v, v_v, w_v, down_v, up_v, tk_ref, tv_ref, len_v, ids_v, len_ref,
    ids_all, attn_all, u_send, u_recv, rs_send, rs_own, rs_recv,
    lora_send, lora_recv, out_send, out_recv, place_v, own_place, lora_sum,
    load_sem, id_ssem, id_rsem, at_ssem, fw_ssem, at_rsem, u_ssem, u_rsem,
    rs_ssem, rs_rsem, lo_ssem, lo_rsem, out_ssem, out_rsem,
):
    z = lax.axis_index("batch")
    t = lax.axis_index("tensor")
    rows, width = out_ref.shape
    n = 4
    held = 4
    rank_width = down_v.shape[0] // held
    slots = lora_send.shape[1]
    quarter = width // n
    half = rows // 2
    piece = rows // PIECES
    span = k_v.shape[0] // rows

    barrier = pltpu.get_barrier_semaphore()
    for i in range(1, n * n):
        other = (z * n + t + i) % (n * n)
        pl.semaphore_signal(
            barrier,
            inc=1,
            device_id={"batch": other // n, "tensor": other % n},
            device_id_type=pl.DeviceIdType.MESH,
        )

    small_loads = [
        pltpu.make_async_copy(len_hbm, len_v, load_sem.at[13]),
        pltpu.make_async_copy(ids_hbm, ids_v, load_sem.at[14]),
        pltpu.make_async_copy(tk_hbm, tk_ref, load_sem.at[15]),
        pltpu.make_async_copy(tv_hbm, tv_ref, load_sem.at[16]),
    ]
    loads = [pltpu.make_async_copy(q_hbm, q_v, load_sem.at[0])]
    for p in range(PIECES):
        part = pl.ds(p * piece * span, piece * span)
        loads.append(pltpu.make_async_copy(k_hbm.at[part], k_v.at[part], load_sem.at[1 + 2 * p]))
        loads.append(pltpu.make_async_copy(v_hbm.at[part], v_v.at[part], load_sem.at[2 + 2 * p]))
    tail_loads = [
        pltpu.make_async_copy(down_hbm, down_v, load_sem.at[17]),
        pltpu.make_async_copy(w_hbm, w_v, load_sem.at[18]),
        pltpu.make_async_copy(up_hbm, up_v, load_sem.at[19]),
    ]
    for load in small_loads + loads:
        load.start()
    for load in small_loads:
        load.wait()

    def by_row(line):
        return jnp.transpose(jnp.broadcast_to(line.astype(F32), (LANES, rows)))

    len_ref[...] = by_row(len_v[...])
    ids_all[z] = by_row(ids_v[...]).astype(BF16)

    def id_copy(i):
        return remote(ids_all.at[z], ids_all.at[z], id_ssem.at[i - 1], id_rsem.at[z], (z + i) % n, t)

    def own_copy(direction, p):
        part = attn_all.at[z, pl.ds(p * piece, piece)]
        to = z + 1 if direction else z - 1
        return remote(part, part, at_ssem.at[direction, p], at_rsem.at[z, p], to, t)

    loads[0].wait()
    for p in range(PIECES):
        loads[1 + 2 * p].wait()
        loads[2 + 2 * p].wait()
        if p == 0:
            for load in tail_loads:
                load.start()

        def step(i, carry):
            r0 = pl.multiple_of(i * STEP_ROWS, STEP_ROWS)
            attend_rows(r0, q_v, k_v, v_v, tk_ref, tv_ref, len_ref, attn_all, z)
            return carry

        per = piece // STEP_ROWS
        lax.fori_loop(p * per, (p + 1) * per, step, 0)
        if p == 0:
            pl.semaphore_wait(barrier, n * n - 1)
            for i in range(1, n):
                id_copy(i).start()

        @pl.when(z < n - 1)
        def _():
            own_copy(1, p).start()

        @pl.when(z > 0)
        def _():
            own_copy(0, p).start()

    blocks = [z, z + 1 - 2 * (z % 2), 2 - z // 2, 3 - 3 * (z // 2)]

    def block_ids(b):
        return ids_all[b].astype(F32)

    def adapter_mask(ids):
        wide = jnp.concatenate([ids, ids], axis=1)
        lane = lax.broadcasted_iota(jnp.int32, wide.shape, 1)
        return wide == (z * held + lane // rank_width).astype(F32)

    def slot_rows(owner):
        return pl.ds(pl.multiple_of(owner * slots, slots), slots)

    def forward(k, p, to):
        b = blocks[k]
        part = attn_all.at[b, pl.ds(p * piece, piece)]
        return remote(part, part, fw_ssem.at[k, p], at_rsem.at[b, p], to, t)

    def u_copy(k, i):
        return remote(
            u_send.at[k], u_recv.at[k, t], u_ssem.at[k, i - 1], u_rsem.at[k, t], z, (t + i) % n
        )

    def rs_copy(k, i):
        return remote(
            rs_send.at[k, i - 1], rs_recv.at[k, t], rs_ssem.at[k, i - 1], rs_rsem.at[k, t],
            z, (t + i) % n,
        )

    def lora_copy(k):
        return remote(
            lora_send.at[k], lora_recv.at[slot_rows(z)], lo_ssem.at[k], lo_rsem.at[z], blocks[k], t
        )

    def out_copy(k):
        return remote(out_send.at[k], out_recv.at[t], out_ssem.at[k], out_rsem.at[t], blocks[k], z)

    middle = (z * (n - 1 - z)) > 0

    def relay_to(k):
        return z - 1 + 2 * (z % 2) if k == 1 else z - 1 + 2 * (z // 2)

    def relay(k, pieces):
        @pl.when(middle)
        def _():
            for p in pieces:
                forward(k, p, z).wait_recv()
                forward(k, p, relay_to(k)).start()

    def main(k):
        b = blocks[k]
        if k > 0:
            @pl.when(jnp.logical_not(middle))
            def _():
                for p in range(PIECES):
                    forward(k, p, z).wait_recv()

        x = attn_all[b]
        ids = block_ids(b)
        u = lax.dot_general(
            x, down_v[...], (((1,), (1,)), ((), ())), preferred_element_type=F32
        )
        u = jnp.where(adapter_mask(ids), u, 0.0)
        u = u[:, :LANES] + u[:, LANES:]
        u = u[:, :rank_width] + u[:, rank_width:]
        u_send[k] = jnp.concatenate([u[:half], u[half:]], axis=1)
        for i in range(1, n):
            u_copy(k, i).start()

        def project(i, carry):
            q = (t + i) % n
            cols = pl.ds(pl.multiple_of(q * quarter, quarter), quarter)
            part = jnp.dot(attn_all[b], w_v[:, cols], preferred_element_type=F32)
            rs_send[k, i - 1] = part.astype(BF16)
            rs_copy(k, i).start()
            return carry

        lax.fori_loop(1, n, project, 0)
        cols = pl.ds(pl.multiple_of(t * quarter, quarter), quarter)
        rs_own[k] = jnp.dot(attn_all[b], w_v[:, cols], preferred_element_type=F32)

    def post(k):
        b = blocks[k]
        total = u_send[k]
        for i in range(1, n):
            src = (t + i) % n
            remote(
                u_recv.at[k, src], u_recv.at[k, src], u_ssem.at[k, i - 1], u_rsem.at[k, src], z, src
            ).wait_recv()
            total = total + u_recv[k, src]
        u = jnp.concatenate([total[:, :rank_width], total[:, rank_width:]], axis=0)
        u = jnp.concatenate([u, u], axis=1)
        u = jnp.concatenate([u, u], axis=1)
        u = jnp.where(adapter_mask(block_ids(b)), u, 0.0).astype(BF16)
        compact = lax.dot_general(
            place_v[k], u, (((0,), (0,)), ((), ())), preferred_element_type=F32
        )[:slots].astype(BF16)
        target = lora_recv.at[slot_rows(z)] if k == 0 else lora_send.at[k]
        for q in range(n):
            cs = slice(q * quarter, (q + 1) * quarter)
            acc = jnp.dot(compact, up_v[:, cs], preferred_element_type=F32)
            target[:, cs] = (adapter_scale * acc).astype(BF16)
        if k > 0:
            lora_copy(k).start()

        sums = rs_own[k]
        for i in range(1, n):
            src = (t + i) % n
            remote(
                rs_recv.at[k, src], rs_recv.at[k, src], rs_ssem.at[k, i - 1], rs_rsem.at[k, src],
                z, src,
            ).wait_recv()
            sums = sums + rs_recv[k, src].astype(F32)
        out_send[k] = sums.astype(BF16)
        if k > 0:
            out_copy(k).start()
        else:

            @pl.when(t != z)
            def _():
                out_copy(0).start()

            @pl.when(t == z)
            def _():
                out_recv[t] = out_send[0]

    for load in tail_loads:
        load.wait()
    main(0)
    for k in range(1, n):
        b = blocks[k]
        remote(ids_all.at[b], ids_all.at[b], id_ssem.at[0], id_rsem.at[b], z, t).wait_recv()
    slot = lax.broadcasted_iota(jnp.int32, (rows, LANES), 1).astype(F32)
    for k in range(n):
        mine, rank = owner_ranks(block_ids(blocks[k]), z, held, rows)
        place_v[k] = jnp.where(mine & (rank == slot), 1.0, 0.0).astype(BF16)
    for p in range(PIECES):
        relay(1, [p])
        relay(2, [p])
    main(1)
    relay(3, range(PIECES // 2))
    post(0)
    relay(3, range(PIECES // 2, PIECES))
    main(2)
    post(1)
    target = jnp.zeros((rows, LANES), F32)
    for o in range(n):
        mine, rank = owner_ranks(block_ids(z), z * 0 + o, held, rows)
        target = jnp.where(mine, rank + o * slots, target)
    wide_slot = lax.broadcasted_iota(jnp.int32, (rows, 2 * LANES), 1).astype(F32)
    own_place[...] = jnp.where(
        jnp.concatenate([target, target], axis=1) == wide_slot, 1.0, 0.0
    ).astype(BF16)
    post(2)
    main(3)
    post(3)

    for k in range(1, n):
        dst = lora_recv.at[slot_rows(blocks[k])]
        remote(dst, dst, lo_ssem.at[k], lo_rsem.at[blocks[k]], z, t).wait_recv()
    for q in range(n):
        cs = slice(q * quarter, (q + 1) * quarter)
        lora_sum[:, cs] = jnp.dot(
            own_place[:, : n * slots], lora_recv[:, cs], preferred_element_type=F32
        )
    for src in range(n):

        def arrive(src=src):
            remote(
                out_recv.at[src], out_recv.at[src], out_ssem.at[0], out_rsem.at[src], z, t
            ).wait_recv()

        pl.when((z - t) * (z - t) + (src - t) * (src - t) > 0)(arrive)
        cs = slice(src * quarter, (src + 1) * quarter)
        out_ref[:, cs] = (out_recv[src].astype(F32) + lora_sum[:, cs]).astype(BF16)

    for i in range(1, n):
        id_copy(i).wait_send()
    for p in range(PIECES):

        @pl.when(z < n - 1)
        def _():
            own_copy(1, p).wait_send()

        @pl.when(z > 0)
        def _():
            own_copy(0, p).wait_send()

        @pl.when(middle)
        def _():
            for k in range(1, n):
                forward(k, p, relay_to(k)).wait_send()

    for k in range(n):
        for i in range(1, n):
            u_copy(k, i).wait_send()
            rs_copy(k, i).wait_send()
        if k > 0:
            lora_copy(k).wait_send()
            out_copy(k).wait_send()
        else:

            @pl.when(t != z)
            def _():
                out_copy(0).wait_send()


def fused_body(
    queries, cached_keys, cached_values, token_key, token_value, lengths, adapter_index,
    output_weight, adapter_down, adapter_up,
):
    rows, width = queries.shape
    span, kv_width = cached_keys.shape[1:]
    n = lax.axis_size("batch")
    held, _, rank_width = adapter_down.shape
    slots = max(2, 2 * rows // n)
    quarter = width // n
    vmem = pl.BlockSpec(memory_space=pltpu.VMEM)
    hbm = pl.BlockSpec(memory_space=pl.ANY)
    dma = pltpu.SemaphoreType.DMA
    flops = 2 * rows * n * width * (width + held * rank_width)
    return pl.pallas_call(
        kernel,
        out_shape=jax.ShapeDtypeStruct((rows, width), BF16),
        in_specs=[hbm] * 10,
        out_specs=vmem,
        scratch_shapes=[
            pltpu.VMEM((rows, width), BF16),
            pltpu.VMEM((rows * span, kv_width), BF16),
            pltpu.VMEM((rows * span, kv_width), BF16),
            pltpu.VMEM(output_weight.shape, BF16),
            pltpu.VMEM((held * rank_width, width), BF16),
            pltpu.VMEM((held * rank_width, width), BF16),
            pltpu.VMEM(token_key.shape, BF16),
            pltpu.VMEM(token_value.shape, BF16),
            pltpu.VMEM((1, rows), jnp.int32),
            pltpu.VMEM((1, rows), jnp.int32),
            pltpu.VMEM((rows, LANES), F32),
            pltpu.VMEM((n, rows, LANES), BF16),
            pltpu.VMEM((n, rows, width), BF16),
            pltpu.VMEM((n, rows // 2, 2 * rank_width), F32),
            pltpu.VMEM((n, n, rows // 2, 2 * rank_width), F32),
            pltpu.VMEM((n, n - 1, rows, quarter), BF16),
            pltpu.VMEM((n, rows, quarter), F32),
            pltpu.VMEM((n, n, rows, quarter), BF16),
            pltpu.VMEM((n, slots, width), BF16),
            pltpu.VMEM((n * slots, width), BF16),
            pltpu.VMEM((n, rows, quarter), BF16),
            pltpu.VMEM((n, rows, quarter), BF16),
            pltpu.VMEM((n, rows, LANES), BF16),
            pltpu.VMEM((rows, 2 * LANES), BF16),
            pltpu.VMEM((rows, width), F32),
            dma((20,)),
            dma((n - 1,)), dma((n,)),
            dma((2, PIECES)), dma((n, PIECES)), dma((n, PIECES)),
            dma((n, n - 1)), dma((n, n)),
            dma((n, n - 1)), dma((n, n)),
            dma((n,)), dma((n,)),
            dma((n,)), dma((n,)),
        ],
        cost_estimate=pl.CostEstimate(
            flops=flops, bytes_accessed=2 * (width * width + 2 * rows * span * kv_width),
            transcendentals=0,
        ),
        compiler_params=pltpu.CompilerParams(
            collective_id=0, has_side_effects=True, vmem_limit_bytes=62 * 2**20
        ),
    )(
        queries,
        cached_keys.reshape(rows * span, kv_width),
        cached_values.reshape(rows * span, kv_width),
        token_key,
        token_value,
        lengths.reshape(1, rows),
        adapter_index.reshape(1, rows),
        output_weight,
        adapter_down.transpose(0, 2, 1).reshape(held * rank_width, width),
        adapter_up.reshape(held * rank_width, width),
    )


def solution(mesh):
    fused = mesh.shape["batch"] == 4 and mesh.shape["tensor"] == 4
    placed = (
        P(("groups", "batch"), "tensor"),
        P(("groups", "batch"), None, "tensor"),
        P(("groups", "batch"), None, "tensor"),
        P(("groups", "batch"), "tensor"),
        P(("groups", "batch"), "tensor"),
        P(("groups", "batch")),
        P(("groups", "batch")),
        P("tensor", "batch"),
        P("batch", "tensor", None),
        P("batch", None, "tensor"),
    )
    return jax.shard_map(
        fused_body if fused else body,
        mesh=mesh,
        in_specs=placed,
        out_specs=P(("groups", "batch"), "tensor"),
        check_vma=False,
    )
```

```python
import jax
import jax.numpy as jnp
from jax import lax
from jax.experimental import pallas as pl
from jax.experimental.pallas import tpu as pltpu
from jax.sharding import PartitionSpec as P

HEAD_SIZE = 128


adapter_scale = 0.25


def finish_output(
    flattened_rows, select_adapter, adapter_down, adapter_up, owner_count, taken_rows
):
    down_factor = jnp.einsum(
        "tj,ojx->tox", flattened_rows, adapter_down, preferred_element_type=jnp.float32
    )
    partial_small = jnp.einsum("sak,sa->sk", down_factor, select_adapter)
    small_product = lax.psum(partial_small, "tensor").astype(jnp.bfloat16)
    up_factor = jnp.einsum(
        "yg,rgo->yro", small_product, adapter_up, preferred_element_type=jnp.float32
    )
    final_result = (adapter_scale * jnp.einsum("czp,cz->cp", up_factor, select_adapter)).astype(
        jnp.bfloat16
    )
    final_result = final_result.reshape(owner_count, taken_rows, final_result.shape[1])
    return lax.all_to_all(final_result, "batch", split_axis=0, concat_axis=0, tiled=True)


def body(
    queries,
    cached_keys,
    cached_values,
    token_key,
    token_value,
    lengths,
    adapter_index,
    output_weight,
    adapter_down,
    adapter_up,
):
    rows = queries.shape[0]
    width = queries.shape[1]
    span = cached_keys.shape[1]
    kv_local = cached_keys.shape[2] // HEAD_SIZE
    group = width // HEAD_SIZE // kv_local
    score_scale = HEAD_SIZE ** (-0.5)
    query_rows = queries.reshape(rows, kv_local, group, HEAD_SIZE)
    keys = cached_keys.reshape(rows, span, kv_local, HEAD_SIZE)
    values = cached_values.reshape(rows, span, kv_local, HEAD_SIZE)
    newest_key = token_key.reshape(rows, kv_local, HEAD_SIZE)
    fresh_value = token_value.reshape(rows, kv_local, HEAD_SIZE)
    scores = (
        jnp.einsum("rkgd,rlkd->rkgl", query_rows, keys, preferred_element_type=jnp.float32)
        * score_scale
    )
    owned_rows = (
        jnp.einsum("rkgd,rkd->rkg", query_rows, newest_key, preferred_element_type=jnp.float32)
        * score_scale
    )
    valid = lax.broadcasted_iota(jnp.int32, (rows, span), 1) < lengths[:, None]
    scores = jnp.where(valid[:, None, None, :], scores, -jnp.inf)
    top = jnp.maximum(jnp.max(scores, axis=-1), owned_rows)
    expo = jnp.exp(scores - top[..., None])
    own_expo = jnp.exp(owned_rows - top)
    total = jnp.sum(expo, axis=-1) + own_expo
    weights = (expo / total[..., None]).astype(jnp.bfloat16)
    own_weight = (own_expo / total).astype(jnp.bfloat16)
    mixed = jnp.einsum("rkgl,rlkd->rkgd", weights, values, preferred_element_type=jnp.float32)
    mixed = (
        mixed
        + own_weight.astype(jnp.float32)[..., None] * fresh_value.astype(jnp.float32)[:, :, None, :]
    )
    attention_output = mixed.reshape(rows, width).astype(jnp.bfloat16)
    owner_count = lax.axis_size("batch")
    held_rows = adapter_down.shape[0]
    slots = max(2, 2 * rows // owner_count)
    table = owner_count * slots
    partial_sums = jnp.dot(
        lax.all_gather(attention_output, "batch", axis=0, tiled=True),
        output_weight,
        preferred_element_type=jnp.float32,
    )
    routed = lax.all_to_all(partial_sums, "batch", split_axis=0, concat_axis=1, tiled=True)
    base_output = lax.psum_scatter(routed, "tensor", scatter_dimension=1, tiled=True)
    owner = adapter_index // held_rows
    local = adapter_index % held_rows
    owner_hot = (owner[:, None] == lax.broadcasted_iota(jnp.int32, (rows, owner_count), 1)).astype(
        jnp.bfloat16
    )
    earlier = (
        lax.broadcasted_iota(jnp.int32, (rows, rows), 0)
        > lax.broadcasted_iota(jnp.int32, (rows, rows), 1)
    ).astype(jnp.bfloat16)
    before = jnp.dot(earlier, owner_hot, preferred_element_type=jnp.float32)
    position = jnp.sum(before * owner_hot.astype(jnp.float32), axis=1).astype(jnp.int32)
    target = owner * slots + position
    place_rows = (target[:, None] == lax.broadcasted_iota(jnp.int32, (rows, table), 1)).astype(
        jnp.bfloat16
    )
    send_rows = jnp.einsum(
        "rs,rf->sf", place_rows, attention_output, preferred_element_type=jnp.float32
    ).astype(jnp.bfloat16)
    marked = jnp.where(place_rows > 0, (local[:, None] + 1).astype(jnp.float32), 0.0)
    send_ids = (jnp.max(marked, axis=0) - 1.0).astype(jnp.bfloat16)
    send_rows = send_rows.reshape(owner_count, slots, width)
    send_ids = send_ids.reshape(owner_count, slots)
    incoming = lax.all_to_all(send_rows, "batch", split_axis=0, concat_axis=0, tiled=True)
    tags = lax.all_to_all(send_ids, "batch", split_axis=0, concat_axis=0, tiled=True)
    taken_rows = incoming.shape[1]
    flattened_rows = incoming.reshape(-1, width)
    flat_tags = tags.reshape(-1).astype(jnp.float32)
    select_local = (
        flat_tags[:, None]
        == lax.broadcasted_iota(jnp.float32, (flattened_rows.shape[0], held_rows), 1)
    ).astype(jnp.float32)
    returned_output = finish_output(
        flattened_rows, select_local, adapter_down, adapter_up, owner_count, taken_rows
    )
    returned_output = returned_output.reshape(table, -1)
    adapter_rows = jnp.dot(place_rows, returned_output, preferred_element_type=jnp.float32)
    return (base_output + adapter_rows).astype(jnp.bfloat16)


F32 = jnp.float32
BF16 = jnp.bfloat16
PIECES = 6
STEP_ROWS = 16
LANES = 128


def remote(src, dst, send_sem, recv_sem, batch, tensor):
    return pltpu.make_async_remote_copy(
        src_ref=src,
        dst_ref=dst,
        send_sem=send_sem,
        recv_sem=recv_sem,
        device_id={"batch": batch, "tensor": tensor},
        device_id_type=pl.DeviceIdType.MESH,
    )


def attend_rows(r0, q_v, k_v, v_v, tk_ref, tv_ref, len_ref, attn_all, z):
    group = 8
    rows = group * STEP_ROWS
    span = 64
    pos_rows = pl.ds(pl.multiple_of(r0 * span, STEP_ROWS * span), STEP_ROWS * span)
    req = pl.ds(r0, STEP_ROWS)
    row = lax.broadcasted_iota(jnp.int32, (rows, LANES), 0)
    lane = lax.broadcasted_iota(jnp.int32, (rows, LANES), 1)
    in_step = row % STEP_ROWS
    pair = in_step // 2
    lens = jnp.concatenate([len_ref[req, :]] * group, axis=0)
    valid = ((in_step % 2) == (lane // span)) & ((lane % span).astype(F32) < lens)
    scale = HEAD_SIZE ** (-0.5)
    for kv in range(2):
        cols = slice(kv * HEAD_SIZE, (kv + 1) * HEAD_SIZE)
        q = jnp.concatenate(
            [
                q_v[req, (kv * group + h) * HEAD_SIZE : (kv * group + h + 1) * HEAD_SIZE]
                for h in range(group)
            ],
            axis=0,
        )
        s = lax.dot_general(
            q, k_v[pos_rows, cols], (((1,), (1,)), ((), ())), preferred_element_type=F32
        )
        c = s[:, :LANES]
        for j in range(1, STEP_ROWS // 2):
            c = jnp.where(pair == j, s[:, j * LANES : (j + 1) * LANES], c)
        c = jnp.where(valid, c * scale, -jnp.inf)
        tk = jnp.concatenate([tk_ref[req, cols].astype(F32)] * group, axis=0)
        own = jnp.sum(q.astype(F32) * tk, axis=1, keepdims=True) * scale
        top = jnp.maximum(jnp.max(c, axis=1, keepdims=True), own)
        e = jnp.exp(c - top)
        own_e = jnp.exp(own - top)
        total = jnp.sum(e, axis=1, keepdims=True) + own_e
        p = e / total
        own_w = (own_e / total).astype(BF16).astype(F32)
        wide = jnp.concatenate(
            [jnp.where(pair == j, p, 0.0).astype(BF16) for j in range(STEP_ROWS // 2)], axis=1
        )
        o = jnp.dot(wide, v_v[pos_rows, cols], preferred_element_type=F32)
        tv = jnp.concatenate([tv_ref[req, cols].astype(F32)] * group, axis=0)
        o = (o + own_w * tv).astype(BF16)
        for h in range(group):
            head = kv * group + h
            attn_all[z, req, head * HEAD_SIZE : (head + 1) * HEAD_SIZE] = o[
                h * STEP_ROWS : (h + 1) * STEP_ROWS
            ]


def kernel(
    q_hbm, k_hbm, v_hbm, tk_hbm, tv_hbm, len_hbm, ids_hbm, w_hbm, down_hbm, up_hbm,
    out_ref,
    q_v, k_v, v_v, w_v, down_v, up_v, up_src, tk_ref, tv_ref, len_v, ids_v, len_ref,
    ids_all, attn_all, u_send, u_recv, rs_send, rs_own, rs_recv,
    u_all, up_all, out_send, out_recv,
    load_sem, id_ssem, id_rsem, at_ssem, fw_ssem, at_rsem, u_ssem, u_rsem,
    rs_ssem, rs_rsem, ua_ssem, ua_rsem, up_ssem, up_rsem, y_ssem, y_rsem, out_ssem, out_rsem,
):
    z = lax.axis_index("batch")
    t = lax.axis_index("tensor")
    rows, width = out_ref.shape
    n = 4
    held = 4
    rank_width = down_v.shape[0] // held
    y = lax.axis_index("groups")
    share = down_v.shape[0] // 2
    quarter = width // n
    half = rows // 2
    piece = rows // PIECES
    span = k_v.shape[0] // rows

    barrier = pltpu.get_barrier_semaphore()
    for i in range(1, n * n):
        other = (z * n + t + i) % (n * n)
        pl.semaphore_signal(
            barrier,
            inc=1,
            device_id={"batch": other // n, "tensor": other % n},
            device_id_type=pl.DeviceIdType.MESH,
        )

    small_loads = [
        pltpu.make_async_copy(len_hbm, len_v, load_sem.at[13]),
        pltpu.make_async_copy(ids_hbm, ids_v, load_sem.at[14]),
        pltpu.make_async_copy(tk_hbm, tk_ref, load_sem.at[15]),
        pltpu.make_async_copy(tv_hbm, tv_ref, load_sem.at[16]),
    ]
    pl.semaphore_signal(
        barrier, inc=1, device_id={"groups": 1 - y}, device_id_type=pl.DeviceIdType.MESH
    )
    loads = [pltpu.make_async_copy(q_hbm, q_v, load_sem.at[0])]
    for p in range(PIECES):
        part = pl.ds(p * piece * span, piece * span)
        loads.append(pltpu.make_async_copy(k_hbm.at[part], k_v.at[part], load_sem.at[1 + 2 * p]))
        loads.append(pltpu.make_async_copy(v_hbm.at[part], v_v.at[part], load_sem.at[2 + 2 * p]))
    tail_loads = [
        pltpu.make_async_copy(down_hbm, down_v, load_sem.at[17]),
        pltpu.make_async_copy(w_hbm, w_v, load_sem.at[18]),
        pltpu.make_async_copy(up_hbm, up_v, load_sem.at[19]),
    ]
    for load in [tail_loads[2]] + small_loads + loads:
        load.start()
    for load in small_loads:
        load.wait()

    def by_row(line):
        return jnp.transpose(jnp.broadcast_to(line.astype(F32), (LANES, rows)))

    len_ref[...] = by_row(len_v[...])
    ids_all[z] = by_row(ids_v[...]).astype(BF16)

    def id_copy(i):
        return remote(ids_all.at[z], ids_all.at[z], id_ssem.at[i - 1], id_rsem.at[z], (z + i) % n, t)

    def own_copy(direction, p):
        part = attn_all.at[z, pl.ds(p * piece, piece)]
        to = z + 1 if direction else z - 1
        return remote(part, part, at_ssem.at[direction, p], at_rsem.at[z, p], to, t)

    loads[0].wait()
    for p in range(PIECES):
        loads[1 + 2 * p].wait()
        loads[2 + 2 * p].wait()
        if p == 0:
            for load in tail_loads[:2]:
                load.start()

        def step(i, carry):
            r0 = pl.multiple_of(i * STEP_ROWS, STEP_ROWS)
            attend_rows(r0, q_v, k_v, v_v, tk_ref, tv_ref, len_ref, attn_all, z)
            return carry

        per = piece // STEP_ROWS
        lax.fori_loop(p * per, (p + 1) * per, step, 0)
        if p == 0:
            pl.semaphore_wait(barrier, n * n)
            for i in range(1, n):
                id_copy(i).start()
            tail_loads[2].wait()

        @pl.when(z < n - 1)
        def _():
            own_copy(1, p).start()

        @pl.when(z > 0)
        def _():
            own_copy(0, p).start()

    def share_rows(owner, group):
        return pl.ds(pl.multiple_of((owner * 2 + group) * share, share), share)

    def up_copy(i):
        q = (t + i) % n
        return remote(
            up_src.at[q], up_all.at[share_rows(z, y)], up_ssem.at[i], up_rsem.at[z], t, q
        )

    def cross_copy(owner, group):
        part = up_all.at[share_rows(owner, group)]
        return pltpu.make_async_remote_copy(
            src_ref=part, dst_ref=part, send_sem=y_ssem.at[owner], recv_sem=y_rsem.at[owner],
            device_id={"groups": 1 - y}, device_id_type=pl.DeviceIdType.MESH,
        )

    mine_up = pl.ds(pl.multiple_of(y * share, share), share)
    for q in range(n):
        up_src[q] = up_v[mine_up, q * quarter : (q + 1) * quarter]
    for i in range(1, n):
        up_copy(i).start()

    @pl.when(t != z)
    def _():
        up_copy(0).start()

    @pl.when(t == z)
    def _():
        up_all[share_rows(z, y), :] = up_src[t]

    def gather_up():
        for o in range(n):
            here = (z - t) * (z - t) + (z - o) * (z - o) > 0

            @pl.when(here)
            def _(o=o):
                part = up_all.at[share_rows(o, y)]
                remote(part, part, up_ssem.at[0], up_rsem.at[o], z, t).wait_recv()

            cross_copy(o, y).start()

    blocks = [z, z + 1 - 2 * (z % 2), 2 - z // 2, 3 - 3 * (z // 2)]

    def block_ids(b):
        return ids_all[b].astype(F32)

    def adapter_mask(ids, owner):
        wide = jnp.concatenate([ids, ids], axis=1)
        lane = lax.broadcasted_iota(jnp.int32, wide.shape, 1)
        return wide == (owner * held + lane // rank_width).astype(F32)

    def forward(k, p, to):
        b = blocks[k]
        part = attn_all.at[b, pl.ds(p * piece, piece)]
        return remote(part, part, fw_ssem.at[k, p], at_rsem.at[b, p], to, t)

    def u_copy(k, i):
        return remote(
            u_send.at[k], u_recv.at[k, t], u_ssem.at[k, i - 1], u_rsem.at[k, t], z, (t + i) % n
        )

    def rs_copy(k, i):
        return remote(
            rs_send.at[k, i - 1], rs_recv.at[blocks[k], t], rs_ssem.at[k, i - 1], rs_rsem.at[blocks[k], t],
            z, (t + i) % n,
        )

    def ua_copy(k, i):
        b = blocks[k]
        part = u_all.at[b, z]
        return remote(part, part, ua_ssem.at[k, i - 1], ua_rsem.at[b, z], (z + i) % n, t)

    def out_copy(b):
        return remote(out_send.at[b], out_recv.at[t], out_ssem.at[b], out_rsem.at[t], b, z)

    middle = (z * (n - 1 - z)) > 0

    def relay_to(k):
        return z - 1 + 2 * (z % 2) if k == 1 else z - 1 + 2 * (z // 2)

    def relay(k, pieces):
        @pl.when(middle)
        def _():
            for p in pieces:
                forward(k, p, z).wait_recv()
                forward(k, p, relay_to(k)).start()

    def main(k):
        b = blocks[k]
        if k > 0:
            @pl.when(jnp.logical_not(middle))
            def _():
                for p in range(PIECES):
                    forward(k, p, z).wait_recv()

        x = attn_all[b]
        ids = block_ids(b)
        u = lax.dot_general(
            x, down_v[...], (((1,), (1,)), ((), ())), preferred_element_type=F32
        )
        u = jnp.where(adapter_mask(ids, z), u, 0.0)
        u = u[:, :LANES] + u[:, LANES:]
        u = u[:, :rank_width] + u[:, rank_width:]
        u_send[k] = jnp.concatenate([u[:half], u[half:]], axis=1)
        for i in range(1, n):
            u_copy(k, i).start()

        def project(i, carry):
            q = (t + i) % n
            cols = pl.ds(pl.multiple_of(q * quarter, quarter), quarter)
            part = jnp.dot(attn_all[b], w_v[:, cols], preferred_element_type=F32)
            rs_send[k, i - 1] = part.astype(BF16)
            rs_copy(k, i).start()
            return carry

        lax.fori_loop(1, n, project, 0)
        cols = pl.ds(pl.multiple_of(t * quarter, quarter), quarter)
        rs_own[b] = jnp.dot(attn_all[b], w_v[:, cols], preferred_element_type=F32)

    def post(k):
        b = blocks[k]
        total = u_send[k]
        for i in range(1, n):
            src = (t + i) % n
            remote(
                u_recv.at[k, src], u_recv.at[k, src], u_ssem.at[k, i - 1], u_rsem.at[k, src], z, src
            ).wait_recv()
            total = total + u_recv[k, src]
        u = jnp.concatenate([total[:, :rank_width], total[:, rank_width:]], axis=0)
        u_all[b, z] = jnp.concatenate([u, u], axis=1).astype(BF16)
        for i in range(1, n):
            ua_copy(k, i).start()

    def finish(b):
        sums = rs_own[b]
        for i in range(1, n):
            src = (t + i) % n
            remote(
                rs_recv.at[b, src], rs_recv.at[b, src], rs_ssem.at[0, i - 1], rs_rsem.at[b, src],
                z, src,
            ).wait_recv()
            sums = sums + rs_recv[b, src].astype(F32)
        for i in range(1, n):
            o = (z + i) % n
            part = u_all.at[b, o]
            remote(part, part, ua_ssem.at[0, i - 1], ua_rsem.at[b, o], o, t).wait_recv()
        ids = block_ids(b)
        picked = []
        for o in range(n):
            uo = u_all[b, o].astype(F32)
            uo = jnp.concatenate([uo, uo], axis=1)
            picked.append(jnp.where(adapter_mask(ids, z * 0 + o), uo, 0.0).astype(BF16))
        acc = jnp.dot(
            jnp.concatenate(picked, axis=1), up_all[...], preferred_element_type=F32
        )
        lora = (adapter_scale * acc).astype(BF16).astype(F32)
        out_send[b] = (sums + lora).astype(BF16)
        away = (b - z) * (b - z) + (t - z) * (t - z) > 0

        @pl.when(away)
        def _():
            out_copy(b).start()

        @pl.when(jnp.logical_not(away))
        def _():
            out_recv[t] = out_send[b]

    for load in tail_loads[:2]:
        load.wait()
    main(0)
    for k in range(1, n):
        b = blocks[k]
        remote(ids_all.at[b], ids_all.at[b], id_ssem.at[0], id_rsem.at[b], z, t).wait_recv()
    for p in range(PIECES):
        relay(1, [p])
        relay(2, [p])
    main(1)
    relay(3, range(PIECES // 2))
    post(0)
    relay(3, range(PIECES // 2, PIECES))
    post(1)
    gather_up()
    main(2)
    post(2)
    for o in range(n):
        cross_copy(o, 1 - y).wait_recv()
    main(3)
    post(3)
    for b in (1, 2, 0, 3):
        finish(b)

    for src in range(n):

        def arrive(src=src):
            remote(
                out_recv.at[src], out_recv.at[src], out_ssem.at[0], out_rsem.at[src], z, t
            ).wait_recv()

        pl.when((z - t) * (z - t) + (src - t) * (src - t) > 0)(arrive)
        cs = slice(src * quarter, (src + 1) * quarter)
        out_ref[:, cs] = out_recv[src]

    for i in range(1, n):
        id_copy(i).wait_send()
    for p in range(PIECES):

        @pl.when(z < n - 1)
        def _():
            own_copy(1, p).wait_send()

        @pl.when(z > 0)
        def _():
            own_copy(0, p).wait_send()

        @pl.when(middle)
        def _():
            for k in range(1, n):
                forward(k, p, relay_to(k)).wait_send()

    for k in range(n):
        for i in range(1, n):
            u_copy(k, i).wait_send()
            rs_copy(k, i).wait_send()
            ua_copy(k, i).wait_send()
        away = (k - z) * (k - z) + (t - z) * (t - z) > 0

        @pl.when(away)
        def _():
            out_copy(k).wait_send()

        cross_copy(k, y).wait_send()

    for i in range(1, n):
        up_copy(i).wait_send()

    @pl.when(t != z)
    def _():
        up_copy(0).wait_send()


def fused_body(
    queries, cached_keys, cached_values, token_key, token_value, lengths, adapter_index,
    output_weight, adapter_down, adapter_up,
):
    rows, width = queries.shape
    span, kv_width = cached_keys.shape[1:]
    n = lax.axis_size("batch")
    held, _, rank_width = adapter_down.shape
    quarter = width // n
    vmem = pl.BlockSpec(memory_space=pltpu.VMEM)
    hbm = pl.BlockSpec(memory_space=pl.ANY)
    dma = pltpu.SemaphoreType.DMA
    flops = 2 * rows * n * width * (width + held * rank_width)
    return pl.pallas_call(
        kernel,
        out_shape=jax.ShapeDtypeStruct((rows, width), BF16),
        in_specs=[hbm] * 10,
        out_specs=vmem,
        scratch_shapes=[
            pltpu.VMEM((rows, width), BF16),
            pltpu.VMEM((rows * span, kv_width), BF16),
            pltpu.VMEM((rows * span, kv_width), BF16),
            pltpu.VMEM(output_weight.shape, BF16),
            pltpu.VMEM((held * rank_width, width), BF16),
            pltpu.VMEM((held * rank_width, width), BF16),
            pltpu.VMEM((n, held * rank_width // 2, quarter), BF16),
            pltpu.VMEM(token_key.shape, BF16),
            pltpu.VMEM(token_value.shape, BF16),
            pltpu.VMEM((1, rows), jnp.int32),
            pltpu.VMEM((1, rows), jnp.int32),
            pltpu.VMEM((rows, LANES), F32),
            pltpu.VMEM((n, rows, LANES), BF16),
            pltpu.VMEM((n, rows, width), BF16),
            pltpu.VMEM((n, rows // 2, 2 * rank_width), F32),
            pltpu.VMEM((n, n, rows // 2, 2 * rank_width), F32),
            pltpu.VMEM((n, n - 1, rows, quarter), BF16),
            pltpu.VMEM((n, rows, quarter), F32),
            pltpu.VMEM((n, n, rows, quarter), BF16),
            pltpu.VMEM((n, n, rows, LANES), BF16),
            pltpu.VMEM((n * held * rank_width, quarter), BF16),
            pltpu.VMEM((n, rows, quarter), BF16),
            pltpu.VMEM((n, rows, quarter), BF16),
            dma((20,)),
            dma((n - 1,)), dma((n,)),
            dma((2, PIECES)), dma((n, PIECES)), dma((n, PIECES)),
            dma((n, n - 1)), dma((n, n)),
            dma((n, n - 1)), dma((n, n)),
            dma((n, n - 1)), dma((n, n)),
            dma((n,)), dma((n,)),
            dma((n,)), dma((n,)),
            dma((n,)), dma((n,)),
        ],
        cost_estimate=pl.CostEstimate(
            flops=flops, bytes_accessed=2 * (width * width + 2 * rows * span * kv_width),
            transcendentals=0,
        ),
        compiler_params=pltpu.CompilerParams(
            collective_id=0, has_side_effects=True, vmem_limit_bytes=62 * 2**20
        ),
    )(
        queries,
        cached_keys.reshape(rows * span, kv_width),
        cached_values.reshape(rows * span, kv_width),
        token_key,
        token_value,
        lengths.reshape(1, rows),
        adapter_index.reshape(1, rows),
        output_weight,
        adapter_down.transpose(0, 2, 1).reshape(held * rank_width, width),
        adapter_up.reshape(held * rank_width, width),
    )


def solution(mesh):
    fused = mesh.shape["batch"] == 4 and mesh.shape["tensor"] == 4 and mesh.shape["groups"] == 2
    placed = (
        P(("groups", "batch"), "tensor"),
        P(("groups", "batch"), None, "tensor"),
        P(("groups", "batch"), None, "tensor"),
        P(("groups", "batch"), "tensor"),
        P(("groups", "batch"), "tensor"),
        P(("groups", "batch")),
        P(("groups", "batch")),
        P("tensor", "batch"),
        P("batch", "tensor", None),
        P("batch", None, "tensor"),
    )
    return jax.shard_map(
        fused_body if fused else body,
        mesh=mesh,
        in_specs=placed,
        out_specs=P(("groups", "batch"), "tensor"),
        check_vma=False,
    )
```

```python
import jax
import jax.numpy as jnp
from jax import lax
from jax.experimental import pallas as pl
from jax.experimental.pallas import tpu as pltpu
from jax.sharding import PartitionSpec as P

HEAD_SIZE = 128


adapter_scale = 0.25


def finish_output(
    flattened_rows, select_adapter, adapter_down, adapter_up, owner_count, taken_rows
):
    down_factor = jnp.einsum(
        "tj,ojx->tox", flattened_rows, adapter_down, preferred_element_type=jnp.float32
    )
    partial_small = jnp.einsum("sak,sa->sk", down_factor, select_adapter)
    small_product = lax.psum(partial_small, "tensor").astype(jnp.bfloat16)
    up_factor = jnp.einsum(
        "yg,rgo->yro", small_product, adapter_up, preferred_element_type=jnp.float32
    )
    final_result = (adapter_scale * jnp.einsum("czp,cz->cp", up_factor, select_adapter)).astype(
        jnp.bfloat16
    )
    final_result = final_result.reshape(owner_count, taken_rows, final_result.shape[1])
    return lax.all_to_all(final_result, "batch", split_axis=0, concat_axis=0, tiled=True)


def body(
    queries,
    cached_keys,
    cached_values,
    token_key,
    token_value,
    lengths,
    adapter_index,
    output_weight,
    adapter_down,
    adapter_up,
):
    rows = queries.shape[0]
    width = queries.shape[1]
    span = cached_keys.shape[1]
    kv_local = cached_keys.shape[2] // HEAD_SIZE
    group = width // HEAD_SIZE // kv_local
    score_scale = HEAD_SIZE ** (-0.5)
    query_rows = queries.reshape(rows, kv_local, group, HEAD_SIZE)
    keys = cached_keys.reshape(rows, span, kv_local, HEAD_SIZE)
    values = cached_values.reshape(rows, span, kv_local, HEAD_SIZE)
    newest_key = token_key.reshape(rows, kv_local, HEAD_SIZE)
    fresh_value = token_value.reshape(rows, kv_local, HEAD_SIZE)
    scores = (
        jnp.einsum("rkgd,rlkd->rkgl", query_rows, keys, preferred_element_type=jnp.float32)
        * score_scale
    )
    owned_rows = (
        jnp.einsum("rkgd,rkd->rkg", query_rows, newest_key, preferred_element_type=jnp.float32)
        * score_scale
    )
    valid = lax.broadcasted_iota(jnp.int32, (rows, span), 1) < lengths[:, None]
    scores = jnp.where(valid[:, None, None, :], scores, -jnp.inf)
    top = jnp.maximum(jnp.max(scores, axis=-1), owned_rows)
    expo = jnp.exp(scores - top[..., None])
    own_expo = jnp.exp(owned_rows - top)
    total = jnp.sum(expo, axis=-1) + own_expo
    weights = (expo / total[..., None]).astype(jnp.bfloat16)
    own_weight = (own_expo / total).astype(jnp.bfloat16)
    mixed = jnp.einsum("rkgl,rlkd->rkgd", weights, values, preferred_element_type=jnp.float32)
    mixed = (
        mixed
        + own_weight.astype(jnp.float32)[..., None] * fresh_value.astype(jnp.float32)[:, :, None, :]
    )
    attention_output = mixed.reshape(rows, width).astype(jnp.bfloat16)
    owner_count = lax.axis_size("batch")
    held_rows = adapter_down.shape[0]
    slots = max(2, 2 * rows // owner_count)
    table = owner_count * slots
    partial_sums = jnp.dot(
        lax.all_gather(attention_output, "batch", axis=0, tiled=True),
        output_weight,
        preferred_element_type=jnp.float32,
    )
    routed = lax.all_to_all(partial_sums, "batch", split_axis=0, concat_axis=1, tiled=True)
    base_output = lax.psum_scatter(routed, "tensor", scatter_dimension=1, tiled=True)
    owner = adapter_index // held_rows
    local = adapter_index % held_rows
    owner_hot = (owner[:, None] == lax.broadcasted_iota(jnp.int32, (rows, owner_count), 1)).astype(
        jnp.bfloat16
    )
    earlier = (
        lax.broadcasted_iota(jnp.int32, (rows, rows), 0)
        > lax.broadcasted_iota(jnp.int32, (rows, rows), 1)
    ).astype(jnp.bfloat16)
    before = jnp.dot(earlier, owner_hot, preferred_element_type=jnp.float32)
    position = jnp.sum(before * owner_hot.astype(jnp.float32), axis=1).astype(jnp.int32)
    target = owner * slots + position
    place_rows = (target[:, None] == lax.broadcasted_iota(jnp.int32, (rows, table), 1)).astype(
        jnp.bfloat16
    )
    send_rows = jnp.einsum(
        "rs,rf->sf", place_rows, attention_output, preferred_element_type=jnp.float32
    ).astype(jnp.bfloat16)
    marked = jnp.where(place_rows > 0, (local[:, None] + 1).astype(jnp.float32), 0.0)
    send_ids = (jnp.max(marked, axis=0) - 1.0).astype(jnp.bfloat16)
    send_rows = send_rows.reshape(owner_count, slots, width)
    send_ids = send_ids.reshape(owner_count, slots)
    incoming = lax.all_to_all(send_rows, "batch", split_axis=0, concat_axis=0, tiled=True)
    tags = lax.all_to_all(send_ids, "batch", split_axis=0, concat_axis=0, tiled=True)
    taken_rows = incoming.shape[1]
    flattened_rows = incoming.reshape(-1, width)
    flat_tags = tags.reshape(-1).astype(jnp.float32)
    select_local = (
        flat_tags[:, None]
        == lax.broadcasted_iota(jnp.float32, (flattened_rows.shape[0], held_rows), 1)
    ).astype(jnp.float32)
    returned_output = finish_output(
        flattened_rows, select_local, adapter_down, adapter_up, owner_count, taken_rows
    )
    returned_output = returned_output.reshape(table, -1)
    adapter_rows = jnp.dot(place_rows, returned_output, preferred_element_type=jnp.float32)
    return (base_output + adapter_rows).astype(jnp.bfloat16)


F32 = jnp.float32
BF16 = jnp.bfloat16
PIECES = 6
STEP_ROWS = 16
LANES = 128


def remote(src, dst, send_sem, recv_sem, batch, tensor):
    return pltpu.make_async_remote_copy(
        src_ref=src,
        dst_ref=dst,
        send_sem=send_sem,
        recv_sem=recv_sem,
        device_id={"batch": batch, "tensor": tensor},
        device_id_type=pl.DeviceIdType.MESH,
    )


def attend_rows(r0, q_v, k_v, v_v, tk_ref, tv_ref, len_ref, attn_all, z):
    group = 8
    rows = group * STEP_ROWS
    span = 64
    pos_rows = pl.ds(pl.multiple_of(r0 * span, STEP_ROWS * span), STEP_ROWS * span)
    req = pl.ds(r0, STEP_ROWS)
    row = lax.broadcasted_iota(jnp.int32, (rows, LANES), 0)
    lane = lax.broadcasted_iota(jnp.int32, (rows, LANES), 1)
    in_step = row % STEP_ROWS
    pair = in_step // 2
    lens = jnp.concatenate([len_ref[req, :]] * group, axis=0)
    valid = ((in_step % 2) == (lane // span)) & ((lane % span).astype(F32) < lens)
    scale = HEAD_SIZE ** (-0.5)
    for kv in range(2):
        cols = slice(kv * HEAD_SIZE, (kv + 1) * HEAD_SIZE)
        q = jnp.concatenate(
            [
                q_v[req, (kv * group + h) * HEAD_SIZE : (kv * group + h + 1) * HEAD_SIZE]
                for h in range(group)
            ],
            axis=0,
        )
        s = lax.dot_general(
            q, k_v[pos_rows, cols], (((1,), (1,)), ((), ())), preferred_element_type=F32
        )
        c = s[:, :LANES]
        for j in range(1, STEP_ROWS // 2):
            c = jnp.where(pair == j, s[:, j * LANES : (j + 1) * LANES], c)
        c = jnp.where(valid, c * scale, -jnp.inf)
        tk = jnp.concatenate([tk_ref[req, cols].astype(F32)] * group, axis=0)
        own = jnp.sum(q.astype(F32) * tk, axis=1, keepdims=True) * scale
        top = jnp.maximum(jnp.max(c, axis=1, keepdims=True), own)
        e = jnp.exp(c - top)
        own_e = jnp.exp(own - top)
        total = jnp.sum(e, axis=1, keepdims=True) + own_e
        p = e / total
        own_w = (own_e / total).astype(BF16).astype(F32)
        wide = jnp.concatenate(
            [jnp.where(pair == j, p, 0.0).astype(BF16) for j in range(STEP_ROWS // 2)], axis=1
        )
        o = jnp.dot(wide, v_v[pos_rows, cols], preferred_element_type=F32)
        tv = jnp.concatenate([tv_ref[req, cols].astype(F32)] * group, axis=0)
        o = (o + own_w * tv).astype(BF16)
        for h in range(group):
            head = kv * group + h
            attn_all[z, req, head * HEAD_SIZE : (head + 1) * HEAD_SIZE] = o[
                h * STEP_ROWS : (h + 1) * STEP_ROWS
            ]


def kernel(
    q_hbm, k_hbm, v_hbm, tk_hbm, tv_hbm, len_hbm, ids_hbm, w_hbm, down_hbm, up_hbm,
    out_ref,
    q_v, k_v, v_v, w_v, down_v, up_v, up_src, tk_ref, tv_ref, len_v, ids_v, len_ref,
    ids_all, attn_all, u_send, u_recv, rs_send, rs_own, rs_recv,
    u_all, up_all, out_send, out_recv,
    load_sem, id_ssem, id_rsem, at_ssem, fw_ssem, at_rsem, u_ssem, u_rsem,
    rs_ssem, rs_rsem, ua_ssem, ua_rsem, up_ssem, up_rsem, y_ssem, y_rsem, out_ssem, out_rsem,
):
    z = lax.axis_index("batch")
    t = lax.axis_index("tensor")
    rows, width = out_ref.shape
    n = 4
    held = 4
    rank_width = down_v.shape[0] // held
    y = lax.axis_index("groups")
    share = down_v.shape[0] // 2
    quarter = width // n
    half = rows // 2
    piece = rows // PIECES
    span = k_v.shape[0] // rows

    barrier = pltpu.get_barrier_semaphore()
    for i in range(1, n * n):
        other = (z * n + t + i) % (n * n)
        pl.semaphore_signal(
            barrier,
            inc=1,
            device_id={"batch": other // n, "tensor": other % n},
            device_id_type=pl.DeviceIdType.MESH,
        )

    small_loads = [
        pltpu.make_async_copy(len_hbm, len_v, load_sem.at[13]),
        pltpu.make_async_copy(ids_hbm, ids_v, load_sem.at[14]),
        pltpu.make_async_copy(tk_hbm, tk_ref, load_sem.at[15]),
        pltpu.make_async_copy(tv_hbm, tv_ref, load_sem.at[16]),
    ]
    pl.semaphore_signal(
        barrier, inc=1, device_id={"groups": 1 - y}, device_id_type=pl.DeviceIdType.MESH
    )
    loads = [pltpu.make_async_copy(q_hbm, q_v, load_sem.at[0])]
    for p in range(PIECES):
        part = pl.ds(p * piece * span, piece * span)
        loads.append(pltpu.make_async_copy(k_hbm.at[part], k_v.at[part], load_sem.at[1 + 2 * p]))
        loads.append(pltpu.make_async_copy(v_hbm.at[part], v_v.at[part], load_sem.at[2 + 2 * p]))
    tail_loads = [
        pltpu.make_async_copy(down_hbm, down_v, load_sem.at[17]),
        pltpu.make_async_copy(w_hbm, w_v, load_sem.at[18]),
        pltpu.make_async_copy(up_hbm, up_v, load_sem.at[19]),
    ]
    for load in [tail_loads[2]] + small_loads + loads:
        load.start()
    for load in small_loads:
        load.wait()

    def by_row(line):
        return jnp.transpose(jnp.broadcast_to(line.astype(F32), (LANES, rows)))

    len_ref[...] = by_row(len_v[...])
    ids_all[z] = by_row(ids_v[...]).astype(BF16)

    def id_copy(i):
        return remote(ids_all.at[z], ids_all.at[z], id_ssem.at[i - 1], id_rsem.at[z], (z + i) % n, t)

    def own_copy(direction, p):
        part = attn_all.at[z, pl.ds(p * piece, piece)]
        to = z + 1 if direction else z - 1
        return remote(part, part, at_ssem.at[direction, p], at_rsem.at[z, p], to, t)

    def share_rows(owner, group):
        return pl.ds(pl.multiple_of((owner * 2 + group) * share, share), share)

    def up_copy(i):
        q = (t + i) % n
        return remote(
            up_src.at[q], up_all.at[share_rows(z, y)], up_ssem.at[i], up_rsem.at[z], t, q
        )

    def cross_copy(owner, group):
        part = up_all.at[share_rows(owner, group)]
        return pltpu.make_async_remote_copy(
            src_ref=part, dst_ref=part, send_sem=y_ssem.at[owner], recv_sem=y_rsem.at[owner],
            device_id={"groups": 1 - y}, device_id_type=pl.DeviceIdType.MESH,
        )

    loads[0].wait()
    for p in range(PIECES):
        loads[1 + 2 * p].wait()
        loads[2 + 2 * p].wait()
        if p == 0:
            for load in tail_loads[:2]:
                load.start()

        def step(i, carry):
            r0 = pl.multiple_of(i * STEP_ROWS, STEP_ROWS)
            attend_rows(r0, q_v, k_v, v_v, tk_ref, tv_ref, len_ref, attn_all, z)
            return carry

        per = piece // STEP_ROWS
        lax.fori_loop(p * per, (p + 1) * per, step, 0)
        if p == 0:
            pl.semaphore_wait(barrier, n * n)
            for i in range(1, n):
                id_copy(i).start()
            tail_loads[2].wait()
            mine_up = pl.ds(pl.multiple_of(y * share, share), share)
            for q in range(n):
                up_src[q] = up_v[mine_up, q * quarter : (q + 1) * quarter]
            for i in range(1, n):
                up_copy(i).start()

            @pl.when(t != z)
            def _():
                up_copy(0).start()

            @pl.when(t == z)
            def _():
                up_all[share_rows(z, y), :] = up_src[t]


        @pl.when(z < n - 1)
        def _():
            own_copy(1, p).start()

        @pl.when(z > 0)
        def _():
            own_copy(0, p).start()

    def gather_up():
        for o in range(n):
            here = (z - t) * (z - t) + (z - o) * (z - o) > 0

            @pl.when(here)
            def _(o=o):
                part = up_all.at[share_rows(o, y)]
                remote(part, part, up_ssem.at[0], up_rsem.at[o], z, t).wait_recv()

            cross_copy(o, y).start()

    blocks = [z, z + 1 - 2 * (z % 2), 2 - z // 2, 3 - 3 * (z // 2)]

    def block_ids(b):
        return ids_all[b].astype(F32)

    def adapter_mask(ids, owner):
        wide = jnp.concatenate([ids, ids], axis=1)
        lane = lax.broadcasted_iota(jnp.int32, wide.shape, 1)
        return wide == (owner * held + lane // rank_width).astype(F32)

    def forward(k, p, to):
        b = blocks[k]
        part = attn_all.at[b, pl.ds(p * piece, piece)]
        return remote(part, part, fw_ssem.at[k, p], at_rsem.at[b, p], to, t)

    def u_copy(k, i):
        return remote(
            u_send.at[k], u_recv.at[k, t], u_ssem.at[k, i - 1], u_rsem.at[k, t], z, (t + i) % n
        )

    def rs_copy(k, i):
        return remote(
            rs_send.at[k, i - 1], rs_recv.at[blocks[k], t], rs_ssem.at[k, i - 1], rs_rsem.at[blocks[k], t],
            z, (t + i) % n,
        )

    def ua_copy(k, i):
        b = blocks[k]
        part = u_all.at[b, z]
        return remote(part, part, ua_ssem.at[k, i - 1], ua_rsem.at[b, z], (z + i) % n, t)

    def out_copy(b):
        return remote(out_send.at[b], out_recv.at[t], out_ssem.at[b], out_rsem.at[t], b, z)

    middle = (z * (n - 1 - z)) > 0

    def relay_to(k):
        return z - 1 + 2 * (z % 2) if k == 1 else z - 1 + 2 * (z // 2)

    def relay(k, pieces):
        @pl.when(middle)
        def _():
            for p in pieces:
                forward(k, p, z).wait_recv()
                forward(k, p, relay_to(k)).start()

    def main(k):
        b = blocks[k]
        if k > 0:
            @pl.when(jnp.logical_not(middle))
            def _():
                for p in range(PIECES):
                    forward(k, p, z).wait_recv()

        x = attn_all[b]
        ids = block_ids(b)
        u = lax.dot_general(
            x, down_v[...], (((1,), (1,)), ((), ())), preferred_element_type=F32
        )
        u = jnp.where(adapter_mask(ids, z), u, 0.0)
        u = u[:, :LANES] + u[:, LANES:]
        u = u[:, :rank_width] + u[:, rank_width:]
        u_send[k] = jnp.concatenate([u[:half], u[half:]], axis=1)
        for i in range(1, n):
            u_copy(k, i).start()

        def project(i, carry):
            q = (t + i) % n
            cols = pl.ds(pl.multiple_of(q * quarter, quarter), quarter)
            part = jnp.dot(attn_all[b], w_v[:, cols], preferred_element_type=F32)
            rs_send[k, i - 1] = part.astype(BF16)
            rs_copy(k, i).start()
            return carry

        lax.fori_loop(1, n, project, 0)
        cols = pl.ds(pl.multiple_of(t * quarter, quarter), quarter)
        rs_own[b] = jnp.dot(attn_all[b], w_v[:, cols], preferred_element_type=F32)

    def post(k):
        b = blocks[k]
        total = u_send[k]
        for i in range(1, n):
            src = (t + i) % n
            remote(
                u_recv.at[k, src], u_recv.at[k, src], u_ssem.at[k, i - 1], u_rsem.at[k, src], z, src
            ).wait_recv()
            total = total + u_recv[k, src]
        u = jnp.concatenate([total[:, :rank_width], total[:, rank_width:]], axis=0)
        u_all[b, z] = jnp.concatenate([u, u], axis=1).astype(BF16)
        for i in range(1, n):
            ua_copy(k, i).start()

    def finish(b):
        sums = rs_own[b]
        for i in range(1, n):
            src = (t + i) % n
            remote(
                rs_recv.at[b, src], rs_recv.at[b, src], rs_ssem.at[0, i - 1], rs_rsem.at[b, src],
                z, src,
            ).wait_recv()
            sums = sums + rs_recv[b, src].astype(F32)
        for i in range(1, n):
            o = (z + i) % n
            part = u_all.at[b, o]
            remote(part, part, ua_ssem.at[0, i - 1], ua_rsem.at[b, o], o, t).wait_recv()
        ids = block_ids(b)
        picked = []
        for o in range(n):
            uo = u_all[b, o].astype(F32)
            uo = jnp.concatenate([uo, uo], axis=1)
            picked.append(jnp.where(adapter_mask(ids, z * 0 + o), uo, 0.0).astype(BF16))
        acc = jnp.dot(
            jnp.concatenate(picked, axis=1), up_all[...], preferred_element_type=F32
        )
        lora = (adapter_scale * acc).astype(BF16).astype(F32)
        out_send[b] = (sums + lora).astype(BF16)
        away = (b - z) * (b - z) + (t - z) * (t - z) > 0

        @pl.when(away)
        def _():
            out_copy(b).start()

        @pl.when(jnp.logical_not(away))
        def _():
            out_recv[t] = out_send[b]

    for load in tail_loads[:2]:
        load.wait()
    main(0)
    for k in range(1, n):
        b = blocks[k]
        remote(ids_all.at[b], ids_all.at[b], id_ssem.at[0], id_rsem.at[b], z, t).wait_recv()
    for p in range(PIECES):
        relay(1, [p])
        relay(2, [p])
    main(1)
    relay(3, range(PIECES // 2))
    post(0)
    relay(3, range(PIECES // 2, PIECES))
    post(1)
    gather_up()
    main(2)
    post(2)
    for o in range(n):
        cross_copy(o, 1 - y).wait_recv()
    finish(1)
    finish(2)
    main(3)
    post(3)
    finish(0)
    finish(3)

    for src in range(n):

        def arrive(src=src):
            remote(
                out_recv.at[src], out_recv.at[src], out_ssem.at[0], out_rsem.at[src], z, t
            ).wait_recv()

        pl.when((z - t) * (z - t) + (src - t) * (src - t) > 0)(arrive)
        cs = slice(src * quarter, (src + 1) * quarter)
        out_ref[:, cs] = out_recv[src]

    for i in range(1, n):
        id_copy(i).wait_send()
    for p in range(PIECES):

        @pl.when(z < n - 1)
        def _():
            own_copy(1, p).wait_send()

        @pl.when(z > 0)
        def _():
            own_copy(0, p).wait_send()

        @pl.when(middle)
        def _():
            for k in range(1, n):
                forward(k, p, relay_to(k)).wait_send()

    for k in range(n):
        for i in range(1, n):
            u_copy(k, i).wait_send()
            rs_copy(k, i).wait_send()
            ua_copy(k, i).wait_send()
        away = (k - z) * (k - z) + (t - z) * (t - z) > 0

        @pl.when(away)
        def _():
            out_copy(k).wait_send()

        cross_copy(k, y).wait_send()

    for i in range(1, n):
        up_copy(i).wait_send()

    @pl.when(t != z)
    def _():
        up_copy(0).wait_send()


def fused_body(
    queries, cached_keys, cached_values, token_key, token_value, lengths, adapter_index,
    output_weight, adapter_down, adapter_up,
):
    rows, width = queries.shape
    span, kv_width = cached_keys.shape[1:]
    n = lax.axis_size("batch")
    held, _, rank_width = adapter_down.shape
    quarter = width // n
    vmem = pl.BlockSpec(memory_space=pltpu.VMEM)
    hbm = pl.BlockSpec(memory_space=pl.ANY)
    dma = pltpu.SemaphoreType.DMA
    flops = 2 * rows * n * width * (width + held * rank_width)
    return pl.pallas_call(
        kernel,
        out_shape=jax.ShapeDtypeStruct((rows, width), BF16),
        in_specs=[hbm] * 10,
        out_specs=vmem,
        scratch_shapes=[
            pltpu.VMEM((rows, width), BF16),
            pltpu.VMEM((rows * span, kv_width), BF16),
            pltpu.VMEM((rows * span, kv_width), BF16),
            pltpu.VMEM(output_weight.shape, BF16),
            pltpu.VMEM((held * rank_width, width), BF16),
            pltpu.VMEM((held * rank_width, width), BF16),
            pltpu.VMEM((n, held * rank_width // 2, quarter), BF16),
            pltpu.VMEM(token_key.shape, BF16),
            pltpu.VMEM(token_value.shape, BF16),
            pltpu.VMEM((1, rows), jnp.int32),
            pltpu.VMEM((1, rows), jnp.int32),
            pltpu.VMEM((rows, LANES), F32),
            pltpu.VMEM((n, rows, LANES), BF16),
            pltpu.VMEM((n, rows, width), BF16),
            pltpu.VMEM((n, rows // 2, 2 * rank_width), F32),
            pltpu.VMEM((n, n, rows // 2, 2 * rank_width), F32),
            pltpu.VMEM((n, n - 1, rows, quarter), BF16),
            pltpu.VMEM((n, rows, quarter), F32),
            pltpu.VMEM((n, n, rows, quarter), BF16),
            pltpu.VMEM((n, n, rows, LANES), BF16),
            pltpu.VMEM((n * held * rank_width, quarter), BF16),
            pltpu.VMEM((n, rows, quarter), BF16),
            pltpu.VMEM((n, rows, quarter), BF16),
            dma((20,)),
            dma((n - 1,)), dma((n,)),
            dma((2, PIECES)), dma((n, PIECES)), dma((n, PIECES)),
            dma((n, n - 1)), dma((n, n)),
            dma((n, n - 1)), dma((n, n)),
            dma((n, n - 1)), dma((n, n)),
            dma((n,)), dma((n,)),
            dma((n,)), dma((n,)),
            dma((n,)), dma((n,)),
        ],
        cost_estimate=pl.CostEstimate(
            flops=flops, bytes_accessed=2 * (width * width + 2 * rows * span * kv_width),
            transcendentals=0,
        ),
        compiler_params=pltpu.CompilerParams(
            collective_id=0, has_side_effects=True, vmem_limit_bytes=62 * 2**20
        ),
    )(
        queries,
        cached_keys.reshape(rows * span, kv_width),
        cached_values.reshape(rows * span, kv_width),
        token_key,
        token_value,
        lengths.reshape(1, rows),
        adapter_index.reshape(1, rows),
        output_weight,
        adapter_down.transpose(0, 2, 1).reshape(held * rank_width, width),
        adapter_up.reshape(held * rank_width, width),
    )


def solution(mesh):
    fused = mesh.shape["batch"] == 4 and mesh.shape["tensor"] == 4 and mesh.shape["groups"] == 2
    placed = (
        P(("groups", "batch"), "tensor"),
        P(("groups", "batch"), None, "tensor"),
        P(("groups", "batch"), None, "tensor"),
        P(("groups", "batch"), "tensor"),
        P(("groups", "batch"), "tensor"),
        P(("groups", "batch")),
        P(("groups", "batch")),
        P("tensor", "batch"),
        P("batch", "tensor", None),
        P("batch", None, "tensor"),
    )
    return jax.shard_map(
        fused_body if fused else body,
        mesh=mesh,
        in_specs=placed,
        out_specs=P(("groups", "batch"), "tensor"),
        check_vma=False,
    )
```
